128 devices in a mesh: src: 8 (over x, core), tgt: 16 (over z, y).
Axes of the slice: x: 4, y: 4, z: 4, core: 2. Of those that a mesh axis runs over, the one named last changes fastest.
Arguments:
- source_fields: float32 [7, 524288], P(None, ('src', 'tgt'))
- slot_source: int32 [8388608], P(('src', 'tgt')), may hold values from 0 to 4095
- slot_weight: float32 [8388608], P(('src', 'tgt')), may hold values from 0.05 to 1
- slot_target: int32 [8388608], P(('src', 'tgt')), may hold values from -1 to 8191, as said below
- cell_mass: float32 [32, 256, 128], P('src', 'tgt'), may hold values from 0.5 to 2
- send_order: int32 [128, 8192], P(('src', 'tgt')), may hold values from 0 to 8191, each once within a row
- place_order: int32 [128, 8192], P(('src', 'tgt')), may hold values from 0 to 8191, each once within a row
Outputs:
- projected: float32 [7, 32, 256, 128], P(None, 'src', 'tgt')
- moduli: float32 [3, 1048576], P(None, ('src', 'tgt'))
The draws below stay inside these ranges and needn't reach their ends.
Inputs may be any that keep to these rules, and one draw needn't show every extreme that they name: `slot_target`: within each sending partition's block of 512 slots at an owner, the live slots come first and there are 128 or more of them; some owner has all 512 slots live from every sender.
All inputs are finite; a program needn't handle non-finite values.
Results may differ from the reference program's by a relative error of at most 0.00007.
Values sent between devices are 32-bit elements; how exact they have to be, the bound alone decides.
A program may use at most 64 MiB of HBM per device.

```python
import math
import jax
import jax.numpy as jnp
from jax import lax

HX = 4
HY = 16
HZ = 128
SC = 4096
CAP = 512
ITERS = 4
OWNERS = 128
TC = 8192
NX = 32
NY = 256
NZ = 128
CELLS = 1048576
NSRC = 524288
SLOTS = 8388608
N_SRC = 8
N_TGT = 16


def draw_source_fields(key, part):
    key = jax.random.fold_in(key, 5)
    k_poro, k_stress = jax.random.split(key, 2)
    poro = jax.random.uniform(k_poro, (1, NSRC), jnp.float32, 0.02, 0.3)
    stress = jax.random.normal(k_stress, (6, NSRC), jnp.float32)
    return jnp.concatenate([poro, stress], axis=0)


def draw_slot_target(key, part):
    key = jax.random.fold_in(key, 2)
    k_count, k_full, k_cell = jax.random.split(key, 3)
    counts = jax.random.randint(k_count, (OWNERS, OWNERS), CAP // 4, CAP + 1)
    full = jax.random.randint(k_full, (), 0, OWNERS)
    owner = jnp.arange(OWNERS, dtype=jnp.int32)[:, None]
    counts = jnp.where(owner == full, CAP, counts)
    cells = jax.random.randint(k_cell, (OWNERS, OWNERS, CAP), 0, TC)
    live = jnp.arange(CAP, dtype=jnp.int32)[None, None, :] < counts[:, :, None]
    return jnp.where(live, cells, -1).astype(jnp.int32).reshape(SLOTS)


def place_ends(result, key, least, high):
    shape = result.shape
    index_at = [jax.random.randint(jax.random.fold_in(key, axis), (), 0, shape[axis]) for axis in range(len(shape))]
    result = result.at[tuple(index_at)].set(least)
    longest = shape.index(max(shape))
    index_at[longest] = (index_at[longest] + 1) % shape[longest]
    return result.at[tuple(index_at)].set(high)


def block_scale(own_key, extent, pieces, least, largest):
    factor_of, own = 1.0, jax.random.fold_in(own_key, 6)
    for axis_at, blocks in pieces:
        steps = jnp.exp(jax.random.uniform(jax.random.fold_in(own, axis_at), (blocks,), jnp.float32, least / len(pieces), largest / len(pieces)))
        factor_of = factor_of * jnp.repeat(steps, extent[axis_at] // blocks).reshape([-1 if axis == axis_at else 1 for axis in range(len(extent))])
    return factor_of


def setup_inputs(seed: int = 0) -> dict:
    key_list = jax.random.split(jax.random.key(seed), 8)
    source_fields = draw_source_fields(jax.random.fold_in(key_list[7], 71), 0)
    slot_source = place_ends(jax.random.randint(key_list[1], (SLOTS,), 0, SC), jax.random.fold_in(key_list[1], 1), 0, SC - 1).astype(jnp.int32)
    slot_weight = jnp.clip(jnp.exp(math.log(1.0) - 2.9957323 * jax.random.uniform(key_list[2], (SLOTS,), jnp.float32) ** block_scale(key_list[2], (SLOTS,), ((0, 128),), -0.2, 0.2)), 0.05, 1.0)
    slot_target = draw_slot_target(jax.random.fold_in(key_list[7], 71), 0)
    cell_mass = jnp.clip(jnp.exp(math.log(2.0) - 1.3862944 * jax.random.uniform(key_list[4], (NX, NY, NZ), jnp.float32) ** block_scale(key_list[4], (NX, NY, NZ), ((0, 8), (1, 16)), -0.2, 0.2)), 0.5, 2.0)
    send_order = jax.vmap(lambda own: jax.random.permutation(own, TC))(jax.random.split(key_list[5], OWNERS)).reshape((OWNERS, TC)).astype(jnp.int32)
    place_order = jax.vmap(lambda own: jax.random.permutation(own, TC))(jax.random.split(key_list[6], OWNERS)).reshape((OWNERS, TC)).astype(jnp.int32)
    return {"source_fields": source_fields, "slot_source": slot_source, "slot_weight": slot_weight, "slot_target": slot_target, "cell_mass": cell_mass, "send_order": send_order, "place_order": place_order}


def mass_apply(field, root):
    w = root[None] * field
    p = jnp.pad(w, ((0, 0), (1, 1), (1, 1), (1, 1)))
    nb = p[:, 2:, 1:-1, 1:-1] + p[:, :-2, 1:-1, 1:-1]
    nb = nb + p[:, 1:-1, 2:, 1:-1] + p[:, 1:-1, :-2, 1:-1]
    nb = nb + p[:, 1:-1, 1:-1, 2:] + p[:, 1:-1, 1:-1, :-2]
    return root[None] * (w + 0.125 * nb)

def cell_moduli(vals):
    phi = vals[0]
    mean = (vals[1] + vals[2] + vals[3]) / 3.0
    q2 = 1.5 * ((vals[1] - mean) ** 2 + (vals[2] - mean) ** 2 + (vals[3] - mean) ** 2 + 2.0 * (vals[4] ** 2 + vals[5] ** 2 + vals[6] ** 2))
    bulk = 1.6 * jnp.exp(-3.0 * phi) * (1.0 + 0.25 * jnp.tanh(mean))
    shear = 0.9 * jnp.exp(-2.0 * phi) / (1.0 + q2 / 0.5)
    soften = shear * q2 / (0.5 + q2)
    return jnp.stack([bulk, shear, soften])

def reference(source_fields, slot_source, slot_weight, slot_target, cell_mass, send_order, place_order):
    fields_by = source_fields.reshape(7, OWNERS, SC).transpose(1, 0, 2)
    src_idx = slot_source.reshape(OWNERS, OWNERS * CAP)
    weights = slot_weight.reshape(OWNERS, OWNERS * CAP)
    tgt = slot_target.reshape(OWNERS, OWNERS, CAP).transpose(1, 0, 2)
    dest = jnp.arange(OWNERS, dtype=jnp.int32)[None, :, None]
    glob = jnp.where(tgt >= 0, dest * TC + tgt, CELLS).astype(jnp.int32).reshape(OWNERS, OWNERS * CAP)

    def add_sender(carry, inputs):
        fld, sidx, wgt, gidx = inputs
        vals = wgt[None, :] * jnp.take(fld, sidx, axis=1)
        return (carry.at[:, gidx].add(vals), None)
    start = jnp.zeros((7, CELLS + 1), jnp.float32)
    total, _ = lax.scan(add_sender, start, (fields_by, src_idx, weights, glob))
    local = total[:, :CELLS].reshape(7, N_SRC, N_TGT, HX, HY, HZ)
    rhs = local.transpose(0, 1, 3, 2, 4, 5).reshape(7, NX, NY, NZ)
    root = jnp.sqrt(cell_mass)
    theta = 1.0
    delta = 0.75
    sigma = theta / delta
    rho = 1.0 / sigma
    x = jnp.zeros_like(rhs)
    r = rhs
    d = r / (theta * cell_mass[None])
    for sweep in range(ITERS):
        image = mass_apply(d, root)
        x = x + d
        r = r - image
        rho_new = 1.0 / (2.0 * sigma - rho)
        d = rho_new * rho * d + 2.0 * rho_new / delta * r / cell_mass[None]
        rho = rho_new
    projected = x + d
    flat = projected.reshape(7, N_SRC, HX, N_TGT, HY, HZ).transpose(0, 1, 3, 2, 4, 5).reshape(7, OWNERS, TC)
    mods = cell_moduli(flat)
    sent = jnp.take_along_axis(mods, send_order[None], axis=2)
    quota = TC // OWNERS
    arrived = sent.reshape(3, OWNERS, OWNERS, quota).transpose(0, 2, 1, 3).reshape(3, OWNERS, TC)
    placed = jnp.take_along_axis(arrived, place_order[None], axis=2)
    return (projected, placed.reshape(3, CELLS))
```

```python
import functools
import math

import jax
import jax.numpy as jnp
from jax import lax
from jax.experimental import pallas as pl
from jax.experimental.pallas import tpu as pltpu
from jax.sharding import PartitionSpec as P

ITERS = 4
MESH = pl.DeviceIdType.MESH
STEP = 2
AHEAD = 8


def gather_pair(fields, source, weight, pair, store):
    rows = pl.ds(pl.multiple_of(8 * pair, 8), 8)
    index = source[rows, :]
    wgt = weight[rows, :]
    lane = index & 127
    group = index >> 7
    bits = [(group & (1 << b)) != 0 for b in range(5)]
    for f in range(7):
        vals = [
            jnp.take_along_axis(
                jnp.broadcast_to(fields[f : f + 1, 128 * r : 128 * r + 128], (8, 128)),
                lane,
                axis=1,
                mode="promise_in_bounds",
            )
            for r in range(32)
        ]
        for bit in bits:
            vals = [jnp.where(bit, vals[2 * j + 1], vals[2 * j]) for j in range(len(vals) // 2)]
        store(f, vals[0] * wgt)


def scatter_pairs(arrived, target, total, pairs):
    iota = lax.broadcasted_iota(jnp.int32, (16, 128), 0).astype(jnp.int16)
    one = jnp.ones((16, 128), jnp.bfloat16)
    zero = jnp.zeros((16, 128), jnp.bfloat16)
    columns, values = [], []
    for slot, pair in pairs:
        for row in range(8):
            half, r = divmod(row, 4)
            cell = jnp.broadcast_to(target[pl.ds(8 * pair + row, 1), :], (16, 128))
            x = cell >> 11
            col = (((x & 1) << 7) + (cell & 127)).astype(jnp.int16)
            up = (((x >> 1) << 4) + ((cell >> 7) & 15)).astype(jnp.int16)
            columns.append(
                jnp.concatenate(
                    [jnp.where(iota == col - jnp.int16(16 * i), one, zero) for i in range(16)], axis=0
                )
            )
            here = [iota == up - jnp.int16(16 * i) for i in range(2)]
            high, low = [], []
            for f in range(7):
                val = jnp.broadcast_to(arrived[2 * slot + half, f, r : r + 1, :], (16, 128))
                top = val.astype(jnp.bfloat16)
                rest = (val - top.astype(jnp.float32)).astype(jnp.bfloat16)
                high += [jnp.where(m, top, zero) for m in here]
                low += [jnp.where(m, rest, zero) for m in here]
            values.append(jnp.concatenate(high + low, axis=0))
    total[...] += lax.dot_general(
        jnp.concatenate(values, axis=1),
        jnp.concatenate(columns, axis=1),
        (((1,), (1,)), ((), ())),
        preferred_element_type=jnp.float32,
    )


def project_kernel(
    n_src, n_tgt, fields, source, weight, target, rhs, outgoing, arrived, total, send_sem, recv_sem
):
    owners = n_src * n_tgt
    pairs = owners // 2
    steps = pairs // STEP
    me = lax.axis_index("src") * n_tgt + lax.axis_index("tgt")
    my_pair, parity = me // 2, me % 2

    barrier = pltpu.get_barrier_semaphore()

    def greet(k):
        other = (me + k) % owners
        pl.semaphore_signal(
            barrier, inc=1, device_id=(other // n_tgt, other % n_tgt), device_id_type=MESH
        )

    def gather(k):
        for u in range(STEP):
            slot = STEP * k + u

            def store(f, val):
                outgoing[2 * slot, f] = val[:4]
                outgoing[2 * slot + 1, f] = val[4:]

            gather_pair(fields, source, weight, (my_pair + slot) % pairs, store)

    def copy(slot, half):
        other = 2 * ((my_pair + slot) % pairs) + half
        return pltpu.make_async_remote_copy(
            src_ref=outgoing.at[2 * slot + half],
            dst_ref=arrived.at[2 * slot + parity],
            send_sem=send_sem.at[2 * slot + half],
            recv_sem=recv_sem.at[2 * slot + parity],
            device_id=(other // n_tgt, other % n_tgt),
            device_id_type=MESH,
        )

    def incoming(slot, half):
        other = 2 * ((my_pair + slot) % pairs) + half
        return pltpu.make_async_remote_copy(
            src_ref=outgoing.at[2 * slot + half],
            dst_ref=arrived.at[2 * slot + half],
            send_sem=send_sem.at[2 * slot + half],
            recv_sem=recv_sem.at[2 * slot + half],
            device_id=(other // n_tgt, other % n_tgt),
            device_id_type=MESH,
        )

    def first(k, carry):
        @pl.when(k > 0)
        def _():
            greet_base = k * (owners // AHEAD)
            for i in range(owners // AHEAD):
                greet(greet_base + i)

        @pl.when(k == 0)
        def _():
            for i in range(1, owners // AHEAD):
                greet(i)

        gather(k)
        return carry

    def launch(k):
        for u in range(STEP):
            for half in range(2):
                copy(STEP * k + u, half).start()

    def take(k):
        for u in range(STEP):
            for half in range(2):
                incoming(STEP * k + u, half).wait_recv()

    def scatter(k):
        scatter_pairs(
            arrived,
            target,
            total,
            [(STEP * k + u, (my_pair - STEP * k - u + pairs) % pairs) for u in range(STEP)],
        )

    total[...] = jnp.zeros_like(total)
    lax.fori_loop(0, AHEAD, first, 0)
    pl.semaphore_wait(barrier, owners - 1)

    copy(0, 1 - parity).start()
    for u in range(1, STEP):
        for half in range(2):
            copy(u, half).start()
    arrived[parity] = outgoing[parity]

    def launch_only(k, carry):
        launch(k)
        return carry

    lax.fori_loop(1, AHEAD, launch_only, 0)

    incoming(0, 1 - parity).wait_recv()
    for u in range(1, STEP):
        for half in range(2):
            incoming(u, half).wait_recv()
    gather(AHEAD)
    scatter(0)
    launch(AHEAD)

    def both(k, carry):
        take(k)
        gather(k + AHEAD)
        scatter(k)
        launch(k + AHEAD)
        return carry

    lax.fori_loop(1, steps - AHEAD, both, 0)

    def last(k, carry):
        take(k)
        scatter(k)
        return carry

    lax.fori_loop(steps - AHEAD, steps, last, 0)

    for f in range(7):
        for x in range(4):
            rows = pl.ds(32 * f + 16 * (x // 2), 16)
            lower = pl.ds(224 + 32 * f + 16 * (x // 2), 16)
            cols = pl.ds(128 * (x % 2), 128)
            rhs[f, x] = total[rows, cols] + total[lower, cols]

    copy(0, 1 - parity).wait_send()

    def drain(k, carry):
        for half in range(2):
            copy(k, half).wait_send()
        return carry

    lax.fori_loop(1, pairs, drain, 0)


def project(source_fields, slot_source, slot_weight, slot_target):
    n_src = lax.axis_size("src")
    n_tgt = lax.axis_size("tgt")
    owners = n_src * n_tgt
    vmem = pl.BlockSpec(memory_space=pltpu.VMEM)
    return pl.pallas_call(
        functools.partial(project_kernel, n_src, n_tgt),
        out_shape=jax.ShapeDtypeStruct((7, 4, 16, 128), jnp.float32),
        in_specs=[vmem] * 4,
        out_specs=vmem,
        scratch_shapes=[
            pltpu.VMEM((owners, 7, 4, 128), jnp.float32),
            pltpu.VMEM((owners, 7, 4, 128), jnp.float32),
            pltpu.VMEM((448, 256), jnp.float32),
            pltpu.SemaphoreType.DMA((owners,)),
            pltpu.SemaphoreType.DMA((owners,)),
        ],
        compiler_params=pltpu.CompilerParams(
            collective_id=0, has_side_effects=True, vmem_limit_bytes=48 << 20
        ),
    )(
        source_fields,
        slot_source.reshape(4 * owners, 128),
        slot_weight.reshape(4 * owners, 128),
        slot_target.reshape(4 * owners, 128),
    )


def padded_2(x, sides, width):
    for axis, dim in sides:
        count, length = (lax.axis_size(axis), x.shape[dim])
        up = [(i, (i + 1) % count) for i in range(count - 1)]
        down = [(j, i) for i, j in up]
        last = lax.slice_in_dim(x, length - width, length, axis=dim)
        first = lax.slice_in_dim(x, 0, width, axis=dim)
        before = lax.ppermute(last, axis, up)
        after = lax.ppermute(first, axis, down)
        x = jnp.concatenate([before, x, after], axis=dim)
    return x


def cell_moduli(vals):
    phi = vals[0]
    mean = (vals[1] + vals[2] + vals[3]) / 3.0
    q2 = 1.5 * (
        (vals[1] - mean) ** 2
        + (vals[2] - mean) ** 2
        + (vals[3] - mean) ** 2
        + 2.0 * (vals[4] ** 2 + vals[5] ** 2 + vals[6] ** 2)
    )
    bulk = 1.6 * jnp.exp(-3.0 * phi) * (1.0 + 0.25 * jnp.tanh(mean))
    shear = 0.9 * jnp.exp(-2.0 * phi) / (1.0 + q2 / 0.5)
    soften = shear * q2 / (0.5 + q2)
    return jnp.stack([bulk, shear, soften])


def lookup_columns(table, index):
    rows, width = table.shape
    groups = width // 32
    folded = table.reshape(rows, groups, 32).transpose(0, 2, 1).reshape(rows * 32, groups)
    count = index.shape[0]
    block = math.gcd(count, 4096)
    group_ids = jnp.arange(groups, dtype=jnp.int32)
    lane_ids = jnp.arange(32, dtype=jnp.int32)

    def one_block(piece):
        onehot = (piece[None, :] // 32 == group_ids[:, None]).astype(jnp.float32)
        picked = jnp.dot(
            folded, onehot, precision=lax.Precision.HIGHEST, preferred_element_type=jnp.float32
        ).reshape(rows, 32, piece.shape[0])
        lanes = (piece[None, :] % 32 == lane_ids[:, None]).astype(jnp.float32)
        return jnp.sum(picked * lanes[None], axis=1)

    pieces = lax.map(one_block, index.reshape(count // block, block))
    return pieces.transpose(1, 0, 2).reshape(rows, count)


def mass_apply(field, root):
    w = root[None] * field
    padded = padded_2(w, (("src", 1), ("tgt", 2)), 1)
    deep = jnp.pad(w, ((0, 0), (0, 0), (0, 0), (1, 1)))
    nb = padded[:, 2:, 1:-1] + padded[:, :-2, 1:-1]
    nb = nb + padded[:, 1:-1, 2:] + padded[:, 1:-1, :-2]
    nb = nb + deep[:, :, :, 2:] + deep[:, :, :, :-2]
    return root[None] * (w + 0.125 * nb)


def on_device(
    source_fields, slot_source, slot_weight, slot_target, cell_mass, send_order, place_order
):
    n_src = lax.axis_size("src")
    n_tgt = lax.axis_size("tgt")
    owners = n_src * n_tgt
    hx_cells, hy_cells, hz_cells = cell_mass.shape
    cells = hx_cells * hy_cells * hz_cells
    quota = cells // owners
    rhs = project(source_fields, slot_source, slot_weight, slot_target)
    root = jnp.sqrt(cell_mass)
    theta = 1.0
    delta = 0.75
    sigma = theta / delta
    rho = 1.0 / sigma
    solution = jnp.zeros_like(rhs)
    resid = rhs
    direction = resid / (theta * cell_mass[None])
    for sweep in range(ITERS):
        image = mass_apply(direction, root)
        solution = solution + direction
        resid = resid - image
        rho_new = 1.0 / (2.0 * sigma - rho)
        direction = rho_new * rho * direction + 2.0 * rho_new / delta * resid / cell_mass[None]
        rho = rho_new
    projected = solution + direction
    flat = projected.reshape(7, cells)
    payload = cell_moduli(flat)
    rows = payload.shape[0]
    outgoing = lookup_columns(payload, send_order[0])
    incoming = lax.all_to_all(
        outgoing.reshape(rows, owners, quota),
        ("src", "tgt"),
        split_axis=1,
        concat_axis=1,
        tiled=True,
    )
    placed = lookup_columns(incoming.reshape(rows, cells), place_order[0])
    return (projected, placed)


def solution(mesh):
    placed = (
        P(None, ("src", "tgt")),
        P(("src", "tgt")),
        P(("src", "tgt")),
        P(("src", "tgt")),
        P("src", "tgt", None),
        P(("src", "tgt"), None),
        P(("src", "tgt"), None),
    )
    return jax.shard_map(
        on_device,
        mesh=mesh,
        in_specs=placed,
        out_specs=(P(None, "src", "tgt", None), P(None, ("src", "tgt"))),
        check_vma=False,
    )
```

```python
import functools

import jax
import jax.numpy as jnp
from jax import lax
from jax.experimental import pallas as pl
from jax.experimental.pallas import tpu as pltpu
from jax.sharding import PartitionSpec as P

ITERS = 4
MESH = pl.DeviceIdType.MESH
STEP = 4
GREET = 4
AHEAD = 8
TURNS = [(1, 0), (-1, 0), (1, 1), (1, -1), (-1, 1), (-1, -1), (0, 1), (0, -1)]


def chebyshev_coefficients():
    def add(p, q, scale=1.0):
        size = max(len(p), len(q))
        p, q = (list(p) + [0.0] * (size - len(p)), list(q) + [0.0] * (size - len(q)))
        return [u + scale * v for u, v in zip(p, q)]

    theta, delta = 1.0, 0.75
    sigma = theta / delta
    rho = 1.0 / sigma
    x, r, d = ([0.0], [1.0], [1.0 / theta])
    for _ in range(ITERS):
        image = add(d, [0.0] + [0.125 * v for v in d])
        x = add(x, d)
        r = add(r, image, -1.0)
        rho_new = 1.0 / (2.0 * sigma - rho)
        d = add([rho_new * rho * v for v in d], [2.0 * rho_new / delta * v for v in r])
        rho = rho_new
    return add(x, d)


def lookup(index, rows, row):
    lane = index & 127
    group = index >> 7

    def tree(low, size):
        if size == 1:
            return jnp.take_along_axis(row(low), lane, axis=1, mode="promise_in_bounds")
        size //= 2
        return jnp.where((group & size) != 0, tree(low + size, size), tree(low, size))

    return tree(0, rows)


def gather_pair(fields, source, weight, pair, store):
    at = pl.ds(pl.multiple_of(8 * pair, 8), 8)
    index = source[at, :]
    wgt = weight[at, :]
    for f in range(7):

        def row(r):
            return jnp.broadcast_to(fields[f : f + 1, 128 * r : 128 * r + 128], (8, 128))

        store(f, lookup(index, 32, row) * wgt)


def scatter_pairs(arrived, target, total, pairs):
    iota = lax.broadcasted_iota(jnp.int32, (16, 128), 0).astype(jnp.int16)
    one = jnp.ones((16, 128), jnp.bfloat16)
    zero = jnp.zeros((16, 128), jnp.bfloat16)
    columns, values = [], []
    for slot, pair in pairs:
        for row in range(8):
            half, r = divmod(row, 4)
            cell = jnp.broadcast_to(target[pl.ds(8 * pair + row, 1), :], (16, 128))
            x = cell >> 11
            col = (((x & 1) << 7) + (cell & 127)).astype(jnp.int16)
            up = (((x >> 1) << 4) + ((cell >> 7) & 15)).astype(jnp.int16)
            columns.append(
                jnp.concatenate(
                    [jnp.where(iota == col - jnp.int16(16 * i), one, zero) for i in range(16)], axis=0
                )
            )
            here = [iota == up - jnp.int16(16 * i) for i in range(2)]
            high, low = [], []
            for f in range(7):
                val = jnp.broadcast_to(arrived[2 * slot + half, f, r : r + 1, :], (16, 128))
                top = val.astype(jnp.bfloat16)
                rest = (val - top.astype(jnp.float32)).astype(jnp.bfloat16)
                high += [jnp.where(m, top, zero) for m in here]
                low += [jnp.where(m, rest, zero) for m in here]
            values.append(jnp.concatenate(high + low, axis=0))
    total[...] += lax.dot_general(
        jnp.concatenate(values, axis=1),
        jnp.concatenate(columns, axis=1),
        (((1,), (1,)), ((), ())),
        preferred_element_type=jnp.float32,
    )


def cell_moduli(vals):
    phi = vals[0]
    mean = (vals[1] + vals[2] + vals[3]) / 3.0
    q2 = 1.5 * (
        (vals[1] - mean) ** 2
        + (vals[2] - mean) ** 2
        + (vals[3] - mean) ** 2
        + 2.0 * (vals[4] ** 2 + vals[5] ** 2 + vals[6] ** 2)
    )
    bulk = 1.6 * jnp.exp(-3.0 * phi) * (1.0 + 0.25 * jnp.tanh(mean))
    shear = 0.9 * jnp.exp(-2.0 * phi) / (1.0 + q2 / 0.5)
    soften = shear * q2 / (0.5 + q2)
    return bulk, shear, soften


def neighbour_sum(before, here, after):
    lane = lax.broadcasted_iota(jnp.int32, here.shape, 1)
    left = jnp.where(lane == 0, 0.0, pltpu.roll(here, 1, 1))
    right = jnp.where(lane == 127, 0.0, pltpu.roll(here, 127, 1))
    rows = here.shape[0]
    return (before + after) + (pltpu.roll(here, 1, 0) + pltpu.roll(here, rows - 1, 0)) + (left + right)


def whole_kernel(
    n_src,
    n_tgt,
    fields_in,
    source_in,
    weight_in,
    target_in,
    mass_in,
    leave_in,
    place_in,
    projected,
    moduli,
    fields,
    source,
    weight,
    target,
    mass,
    leave,
    place,
    outgoing,
    arrived,
    total,
    resid,
    edge,
    beside,
    strips,
    table,
    packed,
    landed,
    load_sem,
    send_sem,
    recv_sem,
    halo_send,
    halo_recv,
    move_send,
    move_recv,
):
    owners = n_src * n_tgt
    pairs = owners // 2
    steps = pairs // STEP
    at_src, at_tgt = lax.axis_index("src"), lax.axis_index("tgt")
    me = at_src * n_tgt + at_tgt
    my_pair, parity = me // 2, me % 2

    loads = [
        pltpu.make_async_copy(a, b, load_sem.at[i])
        for i, (a, b) in enumerate(
            [
                (fields_in, fields),
                (source_in, source),
                (weight_in, weight),
                (target_in, target),
                (mass_in, mass),
                (leave_in, leave),
                (place_in, place),
            ]
        )
    ]
    for load in loads:
        load.start()

    barrier = pltpu.get_barrier_semaphore()

    def greet(k):
        other = (me + k) % owners
        pl.semaphore_signal(
            barrier, inc=1, device_id=(other // n_tgt, other % n_tgt), device_id_type=MESH
        )

    def gather(k):
        for u in range(STEP):
            slot = STEP * k + u

            def store(f, val):
                outgoing[2 * slot, f] = val[:4]
                outgoing[2 * slot + 1, f] = val[4:]

            gather_pair(fields, source, weight, (my_pair + slot) % pairs, store)

    def copy(slot, half, landing):
        other = 2 * ((my_pair + slot) % pairs) + half
        return pltpu.make_async_remote_copy(
            src_ref=outgoing.at[2 * slot + half],
            dst_ref=arrived.at[2 * slot + landing],
            send_sem=send_sem.at[2 * slot + half],
            recv_sem=recv_sem.at[2 * slot + landing],
            device_id=(other // n_tgt, other % n_tgt),
            device_id_type=MESH,
        )

    def each_copy(k, act):
        for u in range(STEP):
            for half in range(2):
                slot = STEP * k + u
                if u == 0:

                    @pl.when((slot > 0) | (parity != half))
                    def _():
                        act(slot, half)

                else:
                    act(slot, half)

    def launch(k):
        each_copy(k, lambda slot, half: copy(slot, half, parity).start())

    def take(k):
        each_copy(k, lambda slot, half: copy(slot, half, half).wait_recv())

    def scatter(k):
        scatter_pairs(
            arrived,
            target,
            total,
            [(STEP * k + u, (my_pair - STEP * k - u + pairs) % pairs) for u in range(STEP)],
        )

    def greet_all(k, carry):
        greet(k)
        return carry

    lax.fori_loop(1, owners, greet_all, 0)
    total[...] = jnp.zeros_like(total)

    @pl.when(at_src == 0)
    def _():
        beside[0] = jnp.zeros_like(beside[0])
        strips[0] = jnp.zeros_like(strips[0])

    @pl.when(at_src == n_src - 1)
    def _():
        beside[1] = jnp.zeros_like(beside[1])
        strips[2] = jnp.zeros_like(strips[2])

    for side, end in ((0, n_tgt - 1), (1, 0)):

        @pl.when(at_tgt == end)
        def _():
            for block in range(3):
                strips[block, side] = jnp.zeros_like(strips[block, side])

    for load in loads:
        load.wait()

    def gather_only(k, carry):
        gather(k)
        return carry

    def launch_only(k, carry):
        launch(k)
        return carry

    def gather_launch(k, carry):
        gather(k)
        launch(k)
        return carry

    def gather_scatter(k, carry):
        take(k)
        gather(k + AHEAD)
        scatter(k)
        launch(k + AHEAD)
        return carry

    def scatter_only(k, carry):
        take(k)
        scatter(k)
        return carry

    lax.fori_loop(0, GREET, gather_only, 0)
    pl.semaphore_wait(barrier, owners - 1)
    lax.fori_loop(0, GREET, launch_only, 0)
    arrived[parity] = outgoing[parity]
    lax.fori_loop(GREET, AHEAD, gather_launch, 0)
    lax.fori_loop(0, steps - AHEAD, gather_scatter, 0)
    lax.fori_loop(steps - AHEAD, steps, scatter_only, 0)

    inverse = [lax.rsqrt(mass[x]) for x in range(4)]
    for f in range(7):
        for x in range(4):
            rows = pl.ds(32 * f + 16 * (x // 2), 16)
            lower = pl.ds(224 + 32 * f + 16 * (x // 2), 16)
            cols = pl.ds(128 * (x % 2), 128)
            val = (total[rows, cols] + total[lower, cols]) * inverse[x]
            resid[f, x] = val
            edge[0, f, x] = val[:4]
            edge[1, f, x] = val[12:]

    def halo(i):
        da, db = TURNS[i]
        if db == 0:
            src, dst = resid, beside.at[0 if da == 1 else 1]
        else:
            side = 1 if db == 1 else 0
            src, dst = edge.at[side], strips.at[1 - da, side]
        return pltpu.make_async_remote_copy(
            src_ref=src,
            dst_ref=dst,
            send_sem=halo_send.at[i],
            recv_sem=halo_recv.at[i],
            device_id=((at_src + da + n_src) % n_src, (at_tgt + db + n_tgt) % n_tgt),
            device_id_type=MESH,
        )

    def inside(i, sign):
        da, db = TURNS[i]
        a, b = at_src + sign * da, at_tgt + sign * db
        return (a >= 0) & (a < n_src) & (b >= 0) & (b < n_tgt)

    for i in range(8):

        @pl.when(inside(i, 1))
        def _():
            halo(i).start()

    for i in range(8):

        @pl.when(inside(i, -1))
        def _():
            halo(i).wait_recv()

    coefs = chebyshev_coefficients()
    row_id = lax.broadcasted_iota(jnp.int32, (24, 128), 0)
    has_next = (at_tgt < n_tgt - 1).astype(jnp.float32)
    has_last = (at_tgt > 0).astype(jnp.float32)
    valid = jnp.where(row_id < 16, 1.0, jnp.where(row_id < 20, has_next, has_last))
    valid_of = [
        valid * (at_src > 0).astype(jnp.float32),
        valid,
        valid * (at_src < n_src - 1).astype(jnp.float32),
    ]

    def sweeps(f, carry):
        planes = []
        for p in range(12):
            block, q = divmod(p, 4)
            main = resid[f, q] if block == 1 else beside[block // 2, f, q]
            planes.append(jnp.concatenate([main, strips[block, 0, f, q], strips[block, 1, f, q]], axis=0))
        state = [coefs[ITERS] * v for v in planes]
        for depth in range(1, ITERS + 1):
            fresh = list(state)
            for p in range(depth, 12 - depth):
                val = neighbour_sum(state[p - 1], state[p], state[p + 1]) + coefs[ITERS - depth] * planes[p]
                fresh[p] = val if depth == ITERS else val * valid_of[p // 4]
            state = fresh
        for x in range(4):
            projected[f, x] = state[4 + x][:16] * inverse[x]
        return carry

    lax.fori_loop(0, 7, sweeps, 0)

    for x in range(4):
        for h in range(2):
            got = cell_moduli([projected[f, x, 8 * h : 8 * h + 8, :] for f in range(7)])
            for m in range(3):
                table[m, 16 * x + 8 * h : 16 * x + 8 * h + 8, :] = got[m]

    lower_half = lax.broadcasted_iota(jnp.int32, (8, 128), 1) < 64

    def swapped(v):
        return pltpu.roll(v, 64, 1)

    def move(sender, other):
        return pltpu.make_async_remote_copy(
            src_ref=packed.at[other],
            dst_ref=landed.at[sender],
            send_sem=move_send.at[other],
            recv_sem=move_recv.at[sender],
            device_id=(other // n_tgt, other % n_tgt),
            device_id_type=MESH,
        )

    def send_group(step, carry):
        group = (step + my_pair // 8) % 8
        index = leave[pl.ds(pl.multiple_of(8 * group, 8), 8), :]
        bulk, shear, soften = [
            lookup(index, 64, lambda r: jnp.broadcast_to(table[m, r : r + 1, :], (8, 128)))
            for m in range(3)
        ]
        even = jnp.full((8, 128), parity, jnp.int32) == 0
        one = jnp.where(even, bulk, shear)
        two = jnp.where(even, shear, bulk)
        soft_swapped = swapped(soften)
        blocks = [
            [jnp.where(lower_half, one, swapped(two)), jnp.where(even, soften, soft_swapped)],
            [jnp.where(lower_half, swapped(one), two), jnp.where(even, soft_swapped, soften)],
        ]
        for i in range(8):
            for half in range(2):
                other = 16 * group + 2 * i + half
                for r in range(2):
                    packed[other, r : r + 1, :] = blocks[half][r][i : i + 1, :]
        for i in range(16):
            other = 16 * group + i

            @pl.when(other != me)
            def _():
                move(me, other).start()

        return carry

    lax.fori_loop(0, 8, send_group, 0)
    landed[me] = packed[me]

    def receive(k, carry):
        sender = (me + k) % owners
        move(sender, sender).wait_recv()
        return carry

    lax.fori_loop(1, owners, receive, 0)

    def fill(step, carry):
        index = place[pl.ds(pl.multiple_of(8 * step, 8), 8), :]

        def row(m, r):
            first, second = [
                jnp.broadcast_to(landed[2 * r + i, m // 2 : m // 2 + 1, :], (8, 128)) for i in range(2)
            ]
            return jnp.where(lower_half, second, first) if m == 1 else jnp.where(lower_half, first, second)

        for m in range(3):
            at = index ^ 64 if m == 1 else index
            moduli[m, pl.ds(pl.multiple_of(8 * step, 8), 8), :] = lookup(at, 64, functools.partial(row, m))
        return carry

    lax.fori_loop(0, 8, fill, 0)

    def drain(k, carry):
        move((me + k) % owners, (me + k) % owners).wait_send()
        return carry

    def drain_copies(k, carry):
        each_copy(k, lambda slot, half: copy(slot, half, half).wait_send())
        return carry

    lax.fori_loop(0, steps, drain_copies, 0)
    lax.fori_loop(1, owners, drain, 0)
    for i in range(8):

        @pl.when(inside(i, 1))
        def _():
            halo(i).wait_send()


def on_device(
    source_fields, slot_source, slot_weight, slot_target, cell_mass, send_order, place_order
):
    n_src = lax.axis_size("src")
    n_tgt = lax.axis_size("tgt")
    owners = n_src * n_tgt
    hx, hy, hz = cell_mass.shape
    cells = hx * hy * hz
    f32, i32 = jnp.float32, jnp.int32
    args = (
        source_fields,
        slot_source.reshape(4 * owners, 128),
        slot_weight.reshape(4 * owners, 128),
        slot_target.reshape(4 * owners, 128),
        cell_mass,
        send_order.reshape(cells // 128, 128),
        place_order.reshape(cells // 128, 128),
    )
    vmem = pl.BlockSpec(memory_space=pltpu.VMEM)
    projected, moduli = pl.pallas_call(
        functools.partial(whole_kernel, n_src, n_tgt),
        out_shape=(
            jax.ShapeDtypeStruct((7, hx, hy, hz), f32),
            jax.ShapeDtypeStruct((3, cells // 128, 128), f32),
        ),
        in_specs=[pl.BlockSpec(memory_space=pltpu.HBM)] * len(args),
        out_specs=(vmem, vmem),
        scratch_shapes=[pltpu.VMEM(a.shape, a.dtype) for a in args]
        + [
            pltpu.VMEM((owners, 7, 4, 128), f32),
            pltpu.VMEM((owners, 7, 4, 128), f32),
            pltpu.VMEM((448, 256), f32),
            pltpu.VMEM((7, hx, hy, hz), f32),
            pltpu.VMEM((2, 7, hx, 4, hz), f32),
            pltpu.VMEM((2, 7, hx, hy, hz), f32),
            pltpu.VMEM((3, 2, 7, hx, 4, hz), f32),
            pltpu.VMEM((3, cells // 128, 128), f32),
            pltpu.VMEM((owners, 2, 128), f32),
            pltpu.VMEM((owners, 2, 128), f32),
            pltpu.SemaphoreType.DMA((len(args),)),
            pltpu.SemaphoreType.DMA((owners,)),
            pltpu.SemaphoreType.DMA((owners,)),
            pltpu.SemaphoreType.DMA((8,)),
            pltpu.SemaphoreType.DMA((8,)),
            pltpu.SemaphoreType.DMA((owners,)),
            pltpu.SemaphoreType.DMA((owners,)),
        ],
        compiler_params=pltpu.CompilerParams(
            collective_id=0, has_side_effects=True, vmem_limit_bytes=60 << 20
        ),
    )(*args)
    return projected, moduli.reshape(3, cells)


def solution(mesh):
    placed = (
        P(None, ("src", "tgt")),
        P(("src", "tgt")),
        P(("src", "tgt")),
        P(("src", "tgt")),
        P("src", "tgt", None),
        P(("src", "tgt"), None),
        P(("src", "tgt"), None),
    )
    return jax.shard_map(
        on_device,
        mesh=mesh,
        in_specs=placed,
        out_specs=(P(None, "src", "tgt", None), P(None, ("src", "tgt"))),
        check_vma=False,
    )
```

```python
import functools

import jax
import jax.numpy as jnp
from jax import lax
from jax.experimental import pallas as pl
from jax.experimental.pallas import tpu as pltpu
from jax.sharding import PartitionSpec as P

ITERS = 4
MESH = pl.DeviceIdType.MESH
STEP = 4
GREET = 4
AHEAD = 8
TURNS = [(1, 0), (-1, 0), (1, 1), (1, -1), (-1, 1), (-1, -1), (0, 1), (0, -1)]


def chebyshev_coefficients():
    def add(p, q, scale=1.0):
        size = max(len(p), len(q))
        p, q = (list(p) + [0.0] * (size - len(p)), list(q) + [0.0] * (size - len(q)))
        return [u + scale * v for u, v in zip(p, q)]

    theta, delta = 1.0, 0.75
    sigma = theta / delta
    rho = 1.0 / sigma
    x, r, d = ([0.0], [1.0], [1.0 / theta])
    for _ in range(ITERS):
        image = add(d, [0.0] + [0.125 * v for v in d])
        x = add(x, d)
        r = add(r, image, -1.0)
        rho_new = 1.0 / (2.0 * sigma - rho)
        d = add([rho_new * rho * v for v in d], [2.0 * rho_new / delta * v for v in r])
        rho = rho_new
    return add(x, d)


def lookup(index, rows, row):
    lane = index & 127
    group = index >> 7

    def tree(low, size):
        if size == 1:
            return jnp.take_along_axis(row(low), lane, axis=1, mode="promise_in_bounds")
        size //= 2
        return jnp.where((group & size) != 0, tree(low + size, size), tree(low, size))

    return tree(0, rows)


def gather_pair(fields, source, weight, pair, store):
    at = pl.ds(pl.multiple_of(8 * pair, 8), 8)
    index = source[at, :]
    wgt = weight[at, :]
    for f in range(7):

        def row(r):
            return jnp.broadcast_to(fields[f : f + 1, 128 * r : 128 * r + 128], (8, 128))

        store(f, lookup(index, 32, row) * wgt)


def scatter_pairs(arrived, target, total, pairs):
    iota = lax.broadcasted_iota(jnp.int32, (16, 128), 0).astype(jnp.int16)
    one = jnp.ones((16, 128), jnp.bfloat16)
    zero = jnp.zeros((16, 128), jnp.bfloat16)
    columns, values = [], []
    for slot, pair in pairs:
        for row in range(8):
            half, r = divmod(row, 4)
            cell = jnp.broadcast_to(target[pl.ds(8 * pair + row, 1), :], (16, 128))
            x = cell >> 11
            col = (((x & 1) << 7) + (cell & 127)).astype(jnp.int16)
            up = (((x >> 1) << 4) + ((cell >> 7) & 15)).astype(jnp.int16)
            columns.append(
                jnp.concatenate(
                    [jnp.where(iota == col - jnp.int16(16 * i), one, zero) for i in range(16)], axis=0
                )
            )
            here = [iota == up - jnp.int16(16 * i) for i in range(2)]
            high, low = [], []
            for f in range(7):
                val = jnp.broadcast_to(arrived[2 * slot + half, f, r : r + 1, :], (16, 128))
                top = val.astype(jnp.bfloat16)
                rest = (val - top.astype(jnp.float32)).astype(jnp.bfloat16)
                high += [jnp.where(m, top, zero) for m in here]
                low += [jnp.where(m, rest, zero) for m in here]
            values.append(jnp.concatenate(high + low, axis=0))
    total[...] += lax.dot_general(
        jnp.concatenate(values, axis=1),
        jnp.concatenate(columns, axis=1),
        (((1,), (1,)), ((), ())),
        preferred_element_type=jnp.float32,
    )


def cell_moduli(vals):
    phi = vals[0]
    mean = (vals[1] + vals[2] + vals[3]) / 3.0
    q2 = 1.5 * (
        (vals[1] - mean) ** 2
        + (vals[2] - mean) ** 2
        + (vals[3] - mean) ** 2
        + 2.0 * (vals[4] ** 2 + vals[5] ** 2 + vals[6] ** 2)
    )
    bulk = 1.6 * jnp.exp(-3.0 * phi) * (1.0 + 0.25 * jnp.tanh(mean))
    shear = 0.9 * jnp.exp(-2.0 * phi) / (1.0 + q2 / 0.5)
    soften = shear * q2 / (0.5 + q2)
    return bulk, shear, soften


def neighbour_sum(before, here, after):
    lane = lax.broadcasted_iota(jnp.int32, here.shape, 1)
    left = jnp.where(lane == 0, 0.0, pltpu.roll(here, 1, 1))
    right = jnp.where(lane == 127, 0.0, pltpu.roll(here, 127, 1))
    rows = here.shape[0]
    return (before + after) + (pltpu.roll(here, 1, 0) + pltpu.roll(here, rows - 1, 0)) + (left + right)


def whole_kernel(
    n_src,
    n_tgt,
    fields_in,
    source_in,
    weight_in,
    target_in,
    mass_in,
    leave_in,
    place_in,
    projected,
    moduli,
    fields,
    source,
    weight,
    target,
    mass,
    leave,
    place,
    outgoing,
    arrived,
    total,
    resid,
    edge,
    beside,
    strips,
    table,
    packed,
    midway,
    landed,
    load_sem,
    send_sem,
    recv_sem,
    halo_send,
    halo_recv,
    across_send,
    across_recv,
    along_send,
    along_recv,
):
    owners = n_src * n_tgt
    pairs = owners // 2
    steps = pairs // STEP
    at_src, at_tgt = lax.axis_index("src"), lax.axis_index("tgt")
    me = at_src * n_tgt + at_tgt
    my_pair, parity = me // 2, me % 2

    loads = [
        pltpu.make_async_copy(a, b, load_sem.at[i])
        for i, (a, b) in enumerate(
            [
                (fields_in, fields),
                (source_in, source),
                (weight_in, weight),
                (target_in, target),
                (mass_in, mass),
                (leave_in, leave),
                (place_in, place),
            ]
        )
    ]
    for load in loads:
        load.start()

    barrier = pltpu.get_barrier_semaphore()

    def gather(k):
        for u in range(STEP):
            slot = STEP * k + u

            def store(f, val):
                outgoing[2 * slot, f] = val[:4]
                outgoing[2 * slot + 1, f] = val[4:]

            gather_pair(fields, source, weight, (my_pair + slot) % pairs, store)

    def copy(slot, half, landing):
        other = 2 * ((my_pair + slot) % pairs) + half
        return pltpu.make_async_remote_copy(
            src_ref=outgoing.at[2 * slot + half],
            dst_ref=arrived.at[2 * slot + landing],
            send_sem=send_sem.at[2 * slot + half],
            recv_sem=recv_sem.at[2 * slot + landing],
            device_id=(other // n_tgt, other % n_tgt),
            device_id_type=MESH,
        )

    def each_copy(k, act):
        for u in range(STEP):
            for half in range(2):
                slot = STEP * k + u
                if u == 0:

                    @pl.when((slot > 0) | (parity != half))
                    def _():
                        act(slot, half)

                else:
                    act(slot, half)

    def launch(k):
        each_copy(k, lambda slot, half: copy(slot, half, parity).start())

    def take(k):
        each_copy(k, lambda slot, half: copy(slot, half, half).wait_recv())

    def scatter(k):
        scatter_pairs(
            arrived,
            target,
            total,
            [(STEP * k + u, (my_pair - STEP * k - u + pairs) % pairs) for u in range(STEP)],
        )

    def greet_row(k, carry):
        row = lax.rem(at_src + k, n_src)
        for j in range(n_tgt):
            pl.semaphore_signal(
                barrier, inc=1, device_id=(row, lax.rem(at_tgt + j, n_tgt)), device_id_type=MESH
            )
        return carry

    for j in range(1, n_tgt):
        pl.semaphore_signal(
            barrier, inc=1, device_id=(at_src, lax.rem(at_tgt + j, n_tgt)), device_id_type=MESH
        )
    lax.fori_loop(1, n_src, greet_row, 0)
    total[...] = jnp.zeros_like(total)

    @pl.when(at_src == 0)
    def _():
        beside[0] = jnp.zeros_like(beside[0])
        strips[0] = jnp.zeros_like(strips[0])

    @pl.when(at_src == n_src - 1)
    def _():
        beside[1] = jnp.zeros_like(beside[1])
        strips[2] = jnp.zeros_like(strips[2])

    for side, end in ((0, n_tgt - 1), (1, 0)):

        @pl.when(at_tgt == end)
        def _():
            for block in range(3):
                strips[block, side] = jnp.zeros_like(strips[block, side])

    for load in loads:
        load.wait()

    def gather_only(k, carry):
        gather(k)
        return carry

    def launch_only(k, carry):
        launch(k)
        return carry

    def gather_launch(k, carry):
        gather(k)
        launch(k)
        return carry

    def gather_scatter(k, carry):
        take(k)
        gather(k + AHEAD)
        scatter(k)
        launch(k + AHEAD)
        return carry

    def scatter_only(k, carry):
        take(k)
        scatter(k)
        return carry

    lax.fori_loop(0, GREET, gather_only, 0)
    pl.semaphore_wait(barrier, owners - 1)
    lax.fori_loop(0, GREET, launch_only, 0)
    arrived[parity] = outgoing[parity]
    lax.fori_loop(GREET, AHEAD, gather_launch, 0)
    lax.fori_loop(0, steps - AHEAD, gather_scatter, 0)
    lax.fori_loop(steps - AHEAD, steps, scatter_only, 0)

    inverse = [lax.rsqrt(mass[x]) for x in range(4)]
    for f in range(7):
        for x in range(4):
            rows = pl.ds(32 * f + 16 * (x // 2), 16)
            lower = pl.ds(224 + 32 * f + 16 * (x // 2), 16)
            cols = pl.ds(128 * (x % 2), 128)
            val = (total[rows, cols] + total[lower, cols]) * inverse[x]
            resid[f, x] = val
            edge[0, f, x] = val[:4]
            edge[1, f, x] = val[12:]

    def halo(i):
        da, db = TURNS[i]
        if db == 0:
            src, dst = resid, beside.at[0 if da == 1 else 1]
        else:
            side = 1 if db == 1 else 0
            src, dst = edge.at[side], strips.at[1 - da, side]
        return pltpu.make_async_remote_copy(
            src_ref=src,
            dst_ref=dst,
            send_sem=halo_send.at[i],
            recv_sem=halo_recv.at[i],
            device_id=((at_src + da + n_src) % n_src, (at_tgt + db + n_tgt) % n_tgt),
            device_id_type=MESH,
        )

    def inside(i, sign):
        da, db = TURNS[i]
        a, b = at_src + sign * da, at_tgt + sign * db
        return (a >= 0) & (a < n_src) & (b >= 0) & (b < n_tgt)

    for i in range(8):

        @pl.when(inside(i, 1))
        def _():
            halo(i).start()

    for i in range(8):

        @pl.when(inside(i, -1))
        def _():
            halo(i).wait_recv()

    coefs = chebyshev_coefficients()
    row_id = lax.broadcasted_iota(jnp.int32, (24, 128), 0)
    has_next = (at_tgt < n_tgt - 1).astype(jnp.float32)
    has_last = (at_tgt > 0).astype(jnp.float32)
    valid = jnp.where(row_id < 16, 1.0, jnp.where(row_id < 20, has_next, has_last))
    valid_of = [
        valid * (at_src > 0).astype(jnp.float32),
        valid,
        valid * (at_src < n_src - 1).astype(jnp.float32),
    ]

    def sweeps(f, carry):
        planes = []
        for p in range(12):
            block, q = divmod(p, 4)
            main = resid[f, q] if block == 1 else beside[block // 2, f, q]
            planes.append(jnp.concatenate([main, strips[block, 0, f, q], strips[block, 1, f, q]], axis=0))
        state = [coefs[ITERS] * v for v in planes]
        for depth in range(1, ITERS + 1):
            fresh = list(state)
            for p in range(depth, 12 - depth):
                val = neighbour_sum(state[p - 1], state[p], state[p + 1]) + coefs[ITERS - depth] * planes[p]
                fresh[p] = val if depth == ITERS else val * valid_of[p // 4]
            state = fresh
        for x in range(4):
            projected[f, x] = state[4 + x][:16] * inverse[x]
        return carry

    lax.fori_loop(0, 7, sweeps, 0)

    for x in range(4):
        for h in range(2):
            got = cell_moduli([projected[f, x, 8 * h : 8 * h + 8, :] for f in range(7)])
            for m in range(3):
                table[m, 16 * x + 8 * h : 16 * x + 8 * h + 8, :] = got[m]

    lower_half = lax.broadcasted_iota(jnp.int32, (8, 128), 1) < 64

    def swapped(v):
        return pltpu.roll(v, 64, 1)

    def across(k):
        other = (at_src + k) % n_src
        return pltpu.make_async_remote_copy(
            src_ref=packed.at[other],
            dst_ref=midway.at[at_src],
            send_sem=across_send.at[k],
            recv_sem=across_recv.at[k],
            device_id=(other, at_tgt),
            device_id_type=MESH,
        )

    def along(k):
        other = (at_tgt + k) % n_tgt
        return pltpu.make_async_remote_copy(
            src_ref=midway.at[:, other],
            dst_ref=landed.at[:, at_tgt],
            send_sem=along_send.at[k],
            recv_sem=along_recv.at[k],
            device_id=(at_src, other),
            device_id_type=MESH,
        )

    def send_group(step, carry):
        group = (step + at_src) % n_src
        index = leave[pl.ds(pl.multiple_of(8 * group, 8), 8), :]
        bulk, shear, soften = [
            lookup(index, 64, lambda r: jnp.broadcast_to(table[m, r : r + 1, :], (8, 128)))
            for m in range(3)
        ]
        even = jnp.full((8, 128), parity, jnp.int32) == 0
        one = jnp.where(even, bulk, shear)
        two = jnp.where(even, shear, bulk)
        soft_swapped = swapped(soften)
        blocks = [
            [jnp.where(lower_half, one, swapped(two)), jnp.where(even, soften, soft_swapped)],
            [jnp.where(lower_half, swapped(one), two), jnp.where(even, soft_swapped, soften)],
        ]
        for i in range(8):
            for half in range(2):
                for r in range(2):
                    packed[group, 2 * i + half, r : r + 1, :] = blocks[half][r][i : i + 1, :]

        @pl.when(step < n_src)
        def _():
            across(step).start()

        return carry

    lax.fori_loop(1, n_src + 1, send_group, 0)
    midway[at_src] = packed[at_src]
    for k in range(1, n_src):
        across(k).wait_recv()
    for k in range(1, n_tgt):
        along(k).start()
    landed[:, at_tgt] = midway[:, at_tgt]
    for k in range(1, n_tgt):
        along(k).wait_recv()

    def fill(step, carry):
        index = place[pl.ds(pl.multiple_of(8 * step, 8), 8), :]

        def row(m, r):
            first, second = [
                jnp.broadcast_to(landed[r // 8, (2 * r + i) % 16, m // 2 : m // 2 + 1, :], (8, 128))
                for i in range(2)
            ]
            return jnp.where(lower_half, second, first) if m == 1 else jnp.where(lower_half, first, second)

        for m in range(3):
            at = index ^ 64 if m == 1 else index
            moduli[m, pl.ds(pl.multiple_of(8 * step, 8), 8), :] = lookup(at, 64, functools.partial(row, m))
        return carry

    lax.fori_loop(0, 8, fill, 0)

    def drain_copies(k, carry):
        each_copy(k, lambda slot, half: copy(slot, half, half).wait_send())
        return carry

    lax.fori_loop(0, steps, drain_copies, 0)
    for k in range(1, n_src):
        across(k).wait_send()
    for k in range(1, n_tgt):
        along(k).wait_send()
    for i in range(8):

        @pl.when(inside(i, 1))
        def _():
            halo(i).wait_send()


def on_device(
    source_fields, slot_source, slot_weight, slot_target, cell_mass, send_order, place_order
):
    n_src = lax.axis_size("src")
    n_tgt = lax.axis_size("tgt")
    owners = n_src * n_tgt
    hx, hy, hz = cell_mass.shape
    cells = hx * hy * hz
    f32, i32 = jnp.float32, jnp.int32
    args = (
        source_fields,
        slot_source.reshape(4 * owners, 128),
        slot_weight.reshape(4 * owners, 128),
        slot_target.reshape(4 * owners, 128),
        cell_mass,
        send_order.reshape(cells // 128, 128),
        place_order.reshape(cells // 128, 128),
    )
    vmem = pl.BlockSpec(memory_space=pltpu.VMEM)
    projected, moduli = pl.pallas_call(
        functools.partial(whole_kernel, n_src, n_tgt),
        out_shape=(
            jax.ShapeDtypeStruct((7, hx, hy, hz), f32),
            jax.ShapeDtypeStruct((3, cells // 128, 128), f32),
        ),
        in_specs=[pl.BlockSpec(memory_space=pltpu.HBM)] * len(args),
        out_specs=(vmem, vmem),
        scratch_shapes=[pltpu.VMEM(a.shape, a.dtype) for a in args]
        + [
            pltpu.VMEM((owners, 7, 4, 128), f32),
            pltpu.VMEM((owners, 7, 4, 128), f32),
            pltpu.VMEM((448, 256), f32),
            pltpu.VMEM((7, hx, hy, hz), f32),
            pltpu.VMEM((2, 7, hx, 4, hz), f32),
            pltpu.VMEM((2, 7, hx, hy, hz), f32),
            pltpu.VMEM((3, 2, 7, hx, 4, hz), f32),
            pltpu.VMEM((3, cells // 128, 128), f32),
            pltpu.VMEM((n_src, n_tgt, 2, 128), f32),
            pltpu.VMEM((n_src, n_tgt, 2, 128), f32),
            pltpu.VMEM((n_src, n_tgt, 2, 128), f32),
            pltpu.SemaphoreType.DMA((len(args),)),
            pltpu.SemaphoreType.DMA((owners,)),
            pltpu.SemaphoreType.DMA((owners,)),
            pltpu.SemaphoreType.DMA((8,)),
            pltpu.SemaphoreType.DMA((8,)),
            pltpu.SemaphoreType.DMA((n_src,)),
            pltpu.SemaphoreType.DMA((n_src,)),
            pltpu.SemaphoreType.DMA((n_tgt,)),
            pltpu.SemaphoreType.DMA((n_tgt,)),
        ],
        compiler_params=pltpu.CompilerParams(
            collective_id=0, has_side_effects=True, vmem_limit_bytes=60 << 20
        ),
    )(*args)
    return projected, moduli.reshape(3, cells)


def solution(mesh):
    placed = (
        P(None, ("src", "tgt")),
        P(("src", "tgt")),
        P(("src", "tgt")),
        P(("src", "tgt")),
        P("src", "tgt", None),
        P(("src", "tgt"), None),
        P(("src", "tgt"), None),
    )
    return jax.shard_map(
        on_device,
        mesh=mesh,
        in_specs=placed,
        out_specs=(P(None, "src", "tgt", None), P(None, ("src", "tgt"))),
        check_vma=False,
    )
```

```python
import functools

import jax
import jax.numpy as jnp
from jax import lax
from jax.experimental import pallas as pl
from jax.experimental.pallas import tpu as pltpu
from jax.sharding import PartitionSpec as P

ITERS = 4
MESH = pl.DeviceIdType.MESH
STEP = 4
GREET = 3
AHEAD = 6
PARTS = [(0, 2), (2, 2), (4, 3)]
TURNS = [(1, 0), (-1, 0), (1, 1), (1, -1), (-1, 1), (-1, -1), (0, 1), (0, -1)]


def chebyshev_coefficients():
    def add(p, q, scale=1.0):
        size = max(len(p), len(q))
        p, q = (list(p) + [0.0] * (size - len(p)), list(q) + [0.0] * (size - len(q)))
        return [u + scale * v for u, v in zip(p, q)]

    theta, delta = 1.0, 0.75
    sigma = theta / delta
    rho = 1.0 / sigma
    x, r, d = ([0.0], [1.0], [1.0 / theta])
    for _ in range(ITERS):
        image = add(d, [0.0] + [0.125 * v for v in d])
        x = add(x, d)
        r = add(r, image, -1.0)
        rho_new = 1.0 / (2.0 * sigma - rho)
        d = add([rho_new * rho * v for v in d], [2.0 * rho_new / delta * v for v in r])
        rho = rho_new
    return add(x, d)


def lookup(index, rows, row):
    lane = index & 127
    group = index >> 7

    def tree(low, size):
        if size == 1:
            return jnp.take_along_axis(row(low), lane, axis=1, mode="promise_in_bounds")
        size //= 2
        return jnp.where((group & size) != 0, tree(low + size, size), tree(low, size))

    return tree(0, rows)


def gather_pair(fields, source, weight, pair, store):
    at = pl.ds(pl.multiple_of(8 * pair, 8), 8)
    index = source[at, :]
    wgt = weight[at, :]
    for f in range(7):

        def row(r):
            return jnp.broadcast_to(fields[f : f + 1, 128 * r : 128 * r + 128], (8, 128))

        store(f, lookup(index, 32, row) * wgt)


def scatter_pairs(arrived, target, total, pairs):
    iota = lax.broadcasted_iota(jnp.int32, (16, 128), 0).astype(jnp.int16)
    one = jnp.ones((16, 128), jnp.bfloat16)
    zero = jnp.zeros((16, 128), jnp.bfloat16)
    columns, values = [], []
    for slot, pair in pairs:
        for row in range(8):
            half, r = divmod(row, 4)
            cell = jnp.broadcast_to(target[pl.ds(8 * pair + row, 1), :], (16, 128))
            x = cell >> 11
            col = (((x & 1) << 7) + (cell & 127)).astype(jnp.int16)
            up = (((x >> 1) << 4) + ((cell >> 7) & 15)).astype(jnp.int16)
            columns.append(
                jnp.concatenate(
                    [jnp.where(iota == col - jnp.int16(16 * i), one, zero) for i in range(16)], axis=0
                )
            )
            here = [iota == up - jnp.int16(16 * i) for i in range(2)]
            high, low = [], []
            for f in range(7):
                val = jnp.broadcast_to(arrived[2 * slot + half, f, r : r + 1, :], (16, 128))
                top = val.astype(jnp.bfloat16)
                rest = (val - top.astype(jnp.float32)).astype(jnp.bfloat16)
                high += [jnp.where(m, top, zero) for m in here]
                low += [jnp.where(m, rest, zero) for m in here]
            values.append(jnp.concatenate(high + low, axis=0))
    total[...] += lax.dot_general(
        jnp.concatenate(values, axis=1),
        jnp.concatenate(columns, axis=1),
        (((1,), (1,)), ((), ())),
        preferred_element_type=jnp.float32,
    )


def cell_moduli(vals):
    phi = vals[0]
    mean = (vals[1] + vals[2] + vals[3]) / 3.0
    q2 = 1.5 * (
        (vals[1] - mean) ** 2
        + (vals[2] - mean) ** 2
        + (vals[3] - mean) ** 2
        + 2.0 * (vals[4] ** 2 + vals[5] ** 2 + vals[6] ** 2)
    )
    bulk = 1.6 * jnp.exp(-3.0 * phi) * (1.0 + 0.25 * jnp.tanh(mean))
    shear = 0.9 * jnp.exp(-2.0 * phi) / (1.0 + q2 / 0.5)
    soften = shear * q2 / (0.5 + q2)
    return bulk, shear, soften


def neighbour_sum(before, here, after):
    lane = lax.broadcasted_iota(jnp.int32, here.shape, 1)
    left = jnp.where(lane == 0, 0.0, pltpu.roll(here, 1, 1))
    right = jnp.where(lane == 127, 0.0, pltpu.roll(here, 127, 1))
    rows = here.shape[0]
    return (before + after) + (pltpu.roll(here, 1, 0) + pltpu.roll(here, rows - 1, 0)) + (left + right)


def whole_kernel(
    n_src,
    n_tgt,
    fields_in,
    source_in,
    weight_in,
    target_in,
    mass_in,
    leave_in,
    projected,
    landed,
    fields,
    source,
    weight,
    target,
    mass,
    leave,
    outgoing,
    arrived,
    total,
    resid,
    edge,
    beside,
    strips,
    table,
    packed,
    midway,
    load_sem,
    send_sem,
    recv_sem,
    halo_send,
    halo_recv,
    across_send,
    across_recv,
    along_send,
    along_recv,
):
    owners = n_src * n_tgt
    pairs = owners // 2
    steps = pairs // STEP
    at_src, at_tgt = lax.axis_index("src"), lax.axis_index("tgt")
    me = at_src * n_tgt + at_tgt
    parity = me % 2

    def pair_at(step, sign):
        row, col = step % n_src, (step // n_src + step) % (n_tgt // 2)
        row = (at_src + sign * row + n_src) % n_src
        col = (at_tgt // 2 + sign * col + n_tgt // 2) % (n_tgt // 2)
        return row * (n_tgt // 2) + col

    loads = [
        pltpu.make_async_copy(a, b, load_sem.at[i])
        for i, (a, b) in enumerate(
            [
                (fields_in, fields),
                (source_in, source),
                (weight_in, weight),
                (target_in, target),
                (mass_in, mass),
                (leave_in, leave),
            ]
        )
    ]
    for load in loads:
        load.start()

    barrier = pltpu.get_barrier_semaphore()

    def gather(k):
        for u in range(STEP):
            slot = STEP * k + u

            def store(f, val):
                outgoing[2 * slot, f] = val[:4]
                outgoing[2 * slot + 1, f] = val[4:]

            gather_pair(fields, source, weight, pair_at(slot, 1), store)

    def copy(slot, half, landing):
        other = 2 * pair_at(slot, 1) + half
        return pltpu.make_async_remote_copy(
            src_ref=outgoing.at[2 * slot + half],
            dst_ref=arrived.at[2 * slot + landing],
            send_sem=send_sem.at[2 * slot + half],
            recv_sem=recv_sem.at[2 * slot + landing],
            device_id=(other // n_tgt, other % n_tgt),
            device_id_type=MESH,
        )

    def each_copy(k, act):
        for u in range(STEP):
            for half in range(2):
                slot = STEP * k + u
                if u == 0:

                    @pl.when((slot > 0) | (parity != half))
                    def _():
                        act(slot, half)

                else:
                    act(slot, half)

    def launch(k):
        each_copy(k, lambda slot, half: copy(slot, half, parity).start())

    def take(k):
        each_copy(k, lambda slot, half: copy(slot, half, half).wait_recv())

    def scatter(k):
        scatter_pairs(
            arrived,
            target,
            total,
            [(STEP * k + u, pair_at(STEP * k + u, -1)) for u in range(STEP)],
        )

    def greet_row(k, carry):
        row = lax.rem(at_src + k, n_src)
        for j in range(n_tgt):
            pl.semaphore_signal(
                barrier, inc=1, device_id=(row, lax.rem(at_tgt + j, n_tgt)), device_id_type=MESH
            )
        return carry

    for j in range(1, n_tgt):
        pl.semaphore_signal(
            barrier, inc=1, device_id=(at_src, lax.rem(at_tgt + j, n_tgt)), device_id_type=MESH
        )
    lax.fori_loop(1, n_src, greet_row, 0)
    total[...] = jnp.zeros_like(total)

    @pl.when(at_src == 0)
    def _():
        beside[0] = jnp.zeros_like(beside[0])
        strips[0] = jnp.zeros_like(strips[0])

    @pl.when(at_src == n_src - 1)
    def _():
        beside[1] = jnp.zeros_like(beside[1])
        strips[2] = jnp.zeros_like(strips[2])

    for side, end in ((0, n_tgt - 1), (1, 0)):

        @pl.when(at_tgt == end)
        def _():
            for block in range(3):
                strips[block, side] = jnp.zeros_like(strips[block, side])

    for load in loads:
        load.wait()

    def gather_only(k, carry):
        gather(k)
        return carry

    def launch_only(k, carry):
        launch(k)
        return carry

    def gather_launch(k, carry):
        gather(k)
        launch(k)
        return carry

    def gather_scatter(k, carry):
        take(k)
        gather(k + AHEAD)
        scatter(k)
        launch(k + AHEAD)
        return carry

    def scatter_only(k, carry):
        take(k)
        scatter(k)
        return carry

    lax.fori_loop(0, GREET, gather_only, 0)
    pl.semaphore_wait(barrier, owners - 1)
    lax.fori_loop(0, GREET, launch_only, 0)
    arrived[parity] = outgoing[parity]
    lax.fori_loop(GREET, AHEAD, gather_launch, 0)
    lax.fori_loop(0, steps - AHEAD, gather_scatter, 0)
    lax.fori_loop(steps - AHEAD, steps, scatter_only, 0)

    inverse = [lax.rsqrt(mass[x]) for x in range(4)]
    def halo(part, i):
        da, db = TURNS[i]
        span = pl.ds(*PARTS[part])
        if db == 0:
            src, dst = resid.at[span], beside.at[0 if da == 1 else 1, span]
        else:
            side = 1 if db == 1 else 0
            src, dst = edge.at[side, span], strips.at[1 - da, side, span]
        return pltpu.make_async_remote_copy(
            src_ref=src,
            dst_ref=dst,
            send_sem=halo_send.at[8 * part + i],
            recv_sem=halo_recv.at[8 * part + i],
            device_id=((at_src + da + n_src) % n_src, (at_tgt + db + n_tgt) % n_tgt),
            device_id_type=MESH,
        )

    def inside(i, sign):
        da, db = TURNS[i]
        a, b = at_src + sign * da, at_tgt + sign * db
        return (a >= 0) & (a < n_src) & (b >= 0) & (b < n_tgt)

    def each_halo(part, sign, act):
        for i in range(8):

            @pl.when(inside(i, sign))
            def _():
                act(halo(part, i))

    for part, (first, count) in enumerate(PARTS):
        for f in range(first, first + count):
            for x in range(4):
                rows = pl.ds(32 * f + 16 * (x // 2), 16)
                lower = pl.ds(224 + 32 * f + 16 * (x // 2), 16)
                cols = pl.ds(128 * (x % 2), 128)
                val = (total[rows, cols] + total[lower, cols]) * inverse[x]
                resid[f, x] = val
                edge[0, f, x] = val[:4]
                edge[1, f, x] = val[12:]
        each_halo(part, 1, lambda sent: sent.start())

    def drain_copies(k, carry):
        each_copy(k, lambda slot, half: copy(slot, half, half).wait_send())
        return carry

    lax.fori_loop(0, steps, drain_copies, 0)
    coefs = chebyshev_coefficients()
    row_id = lax.broadcasted_iota(jnp.int32, (24, 128), 0)
    has_next = (at_tgt < n_tgt - 1).astype(jnp.float32)
    has_last = (at_tgt > 0).astype(jnp.float32)
    valid = jnp.where(row_id < 16, 1.0, jnp.where(row_id < 20, has_next, has_last))
    valid_of = [
        valid * (at_src > 0).astype(jnp.float32),
        valid,
        valid * (at_src < n_src - 1).astype(jnp.float32),
    ]

    def sweeps(f, carry):
        planes = []
        for p in range(12):
            block, q = divmod(p, 4)
            main = resid[f, q] if block == 1 else beside[block // 2, f, q]
            planes.append(jnp.concatenate([main, strips[block, 0, f, q], strips[block, 1, f, q]], axis=0))
        state = [coefs[ITERS] * v for v in planes]
        for depth in range(1, ITERS + 1):
            fresh = list(state)
            for p in range(depth, 12 - depth):
                val = neighbour_sum(state[p - 1], state[p], state[p + 1]) + coefs[ITERS - depth] * planes[p]
                fresh[p] = val if depth == ITERS else val * valid_of[p // 4]
            state = fresh
        for x in range(4):
            projected[f, x] = state[4 + x][:16] * inverse[x]
        return carry

    for part, (first, count) in enumerate(PARTS):
        each_halo(part, -1, lambda came: came.wait_recv())
        lax.fori_loop(first, first + count, sweeps, 0)

    for x in range(4):
        for h in range(2):
            got = cell_moduli([projected[f, x, 8 * h : 8 * h + 8, :] for f in range(7)])
            for m in range(3):
                table[m, 16 * x + 8 * h : 16 * x + 8 * h + 8, :] = got[m]

    lower_half = lax.broadcasted_iota(jnp.int32, (8, 128), 1) < 64

    def swapped(v):
        return pltpu.roll(v, 64, 1)

    def across(k):
        other = (at_src + k) % n_src
        return pltpu.make_async_remote_copy(
            src_ref=packed.at[other],
            dst_ref=midway.at[at_src],
            send_sem=across_send.at[k],
            recv_sem=across_recv.at[k],
            device_id=(other, at_tgt),
            device_id_type=MESH,
        )

    def along(k):
        other = (at_tgt + k) % n_tgt
        return pltpu.make_async_remote_copy(
            src_ref=midway.at[:, other],
            dst_ref=landed.at[:, at_tgt],
            send_sem=along_send.at[k],
            recv_sem=along_recv.at[k],
            device_id=(at_src, other),
            device_id_type=MESH,
        )

    def send_group(step, carry):
        group = (step + at_src) % n_src
        index = leave[pl.ds(pl.multiple_of(8 * group, 8), 8), :]
        bulk, shear, soften = [
            lookup(index, 64, lambda r: jnp.broadcast_to(table[m, r : r + 1, :], (8, 128)))
            for m in range(3)
        ]
        even = jnp.full((8, 128), parity, jnp.int32) == 0
        one = jnp.where(even, bulk, shear)
        two = jnp.where(even, shear, bulk)
        soft_swapped = swapped(soften)
        blocks = [
            [jnp.where(lower_half, one, swapped(two)), jnp.where(even, soften, soft_swapped)],
            [jnp.where(lower_half, swapped(one), two), jnp.where(even, soft_swapped, soften)],
        ]
        for i in range(8):
            for half in range(2):
                for r in range(2):
                    packed[group, 2 * i + half, r : r + 1, :] = blocks[half][r][i : i + 1, :]

        @pl.when(step < n_src)
        def _():
            across(step).start()

        return carry

    lax.fori_loop(1, n_src + 1, send_group, 0)
    midway[at_src] = packed[at_src]
    for k in range(1, n_src):
        across(k).wait_recv()
    for k in range(1, n_tgt):
        along(k).start()
    landed[:, at_tgt] = midway[:, at_tgt]
    for k in range(1, n_tgt):
        along(k).wait_recv()

    for k in range(1, n_src):
        across(k).wait_send()
    for k in range(1, n_tgt):
        along(k).wait_send()
    for part in range(len(PARTS)):
        each_halo(part, 1, lambda sent: sent.wait_send())


def place_kernel(landed, place, projected_in, projected, moduli):
    projected[...] = projected_in[...]
    lower_half = lax.broadcasted_iota(jnp.int32, (8, 128), 1) < 64

    def fill(step, carry):
        index = place[pl.ds(pl.multiple_of(8 * step, 8), 8), :]

        def row(m, r):
            first, second = [
                jnp.broadcast_to(landed[r // 8, (2 * r + i) % 16, m // 2 : m // 2 + 1, :], (8, 128))
                for i in range(2)
            ]
            return jnp.where(lower_half, second, first) if m == 1 else jnp.where(lower_half, first, second)

        for m in range(3):
            at = index ^ 64 if m == 1 else index
            got = lookup(at, 64, functools.partial(row, m))
            for i in range(8):
                moduli[m : m + 1, pl.ds(pl.multiple_of(1024 * step + 128 * i, 128), 128)] = got[i : i + 1]
        return carry

    lax.fori_loop(0, 8, fill, 0)


def on_device(
    source_fields, slot_source, slot_weight, slot_target, cell_mass, send_order, place_order
):
    n_src = lax.axis_size("src")
    n_tgt = lax.axis_size("tgt")
    owners = n_src * n_tgt
    hx, hy, hz = cell_mass.shape
    cells = hx * hy * hz
    f32, i32 = jnp.float32, jnp.int32
    args = (
        source_fields,
        slot_source.reshape(4 * owners, 128),
        slot_weight.reshape(4 * owners, 128),
        slot_target.reshape(4 * owners, 128),
        cell_mass,
        send_order.reshape(cells // 128, 128),
    )
    vmem = pl.BlockSpec(memory_space=pltpu.VMEM)
    computed, landed = pl.pallas_call(
        functools.partial(whole_kernel, n_src, n_tgt),
        out_shape=(
            jax.ShapeDtypeStruct((7, hx, hy, hz), f32),
            jax.ShapeDtypeStruct((n_src, n_tgt, 2, 128), f32),
        ),
        in_specs=[pl.BlockSpec(memory_space=pltpu.HBM)] * len(args),
        out_specs=(vmem, vmem),
        scratch_shapes=[pltpu.VMEM(a.shape, a.dtype) for a in args]
        + [
            pltpu.VMEM((owners, 7, 4, 128), f32),
            pltpu.VMEM((owners, 7, 4, 128), f32),
            pltpu.VMEM((448, 256), f32),
            pltpu.VMEM((7, hx, hy, hz), f32),
            pltpu.VMEM((2, 7, hx, 4, hz), f32),
            pltpu.VMEM((2, 7, hx, hy, hz), f32),
            pltpu.VMEM((3, 2, 7, hx, 4, hz), f32),
            pltpu.VMEM((3, cells // 128, 128), f32),
            pltpu.VMEM((n_src, n_tgt, 2, 128), f32),
            pltpu.VMEM((n_src, n_tgt, 2, 128), f32),
            pltpu.SemaphoreType.DMA((len(args),)),
            pltpu.SemaphoreType.DMA((owners,)),
            pltpu.SemaphoreType.DMA((owners,)),
            pltpu.SemaphoreType.DMA((8 * len(PARTS),)),
            pltpu.SemaphoreType.DMA((8 * len(PARTS),)),
            pltpu.SemaphoreType.DMA((n_src,)),
            pltpu.SemaphoreType.DMA((n_src,)),
            pltpu.SemaphoreType.DMA((n_tgt,)),
            pltpu.SemaphoreType.DMA((n_tgt,)),
        ],
        compiler_params=pltpu.CompilerParams(
            collective_id=0, has_side_effects=True, vmem_limit_bytes=60 << 20
        ),
    )(*args)
    return pl.pallas_call(
        place_kernel,
        out_shape=(
            jax.ShapeDtypeStruct((7, hx, hy, hz), f32),
            jax.ShapeDtypeStruct((3, cells), f32),
        ),
        in_specs=(vmem, vmem, vmem),
        out_specs=(vmem, vmem),
    )(landed, place_order.reshape(cells // 128, 128), computed)


def solution(mesh):
    placed = (
        P(None, ("src", "tgt")),
        P(("src", "tgt")),
        P(("src", "tgt")),
        P(("src", "tgt")),
        P("src", "tgt", None),
        P(("src", "tgt"), None),
        P(("src", "tgt"), None),
    )
    return jax.shard_map(
        on_device,
        mesh=mesh,
        in_specs=placed,
        out_specs=(P(None, "src", "tgt", None), P(None, ("src", "tgt"))),
        check_vma=False,
    )
```

```python
import functools

import jax
import jax.numpy as jnp
from jax import lax
from jax.experimental import pallas as pl
from jax.experimental.pallas import tpu as pltpu
from jax.sharding import PartitionSpec as P

ITERS = 4
MESH = pl.DeviceIdType.MESH
STEP = 4
GREET = 3
AHEAD = 6
PARTS = [(0, 2), (2, 2), (4, 3)]
TURNS = [(1, 0), (-1, 0), (1, 1), (1, -1), (-1, 1), (-1, -1), (0, 1), (0, -1)]


def chebyshev_coefficients():
    def add(p, q, scale=1.0):
        size = max(len(p), len(q))
        p, q = (list(p) + [0.0] * (size - len(p)), list(q) + [0.0] * (size - len(q)))
        return [u + scale * v for u, v in zip(p, q)]

    theta, delta = 1.0, 0.75
    sigma = theta / delta
    rho = 1.0 / sigma
    x, r, d = ([0.0], [1.0], [1.0 / theta])
    for _ in range(ITERS):
        image = add(d, [0.0] + [0.125 * v for v in d])
        x = add(x, d)
        r = add(r, image, -1.0)
        rho_new = 1.0 / (2.0 * sigma - rho)
        d = add([rho_new * rho * v for v in d], [2.0 * rho_new / delta * v for v in r])
        rho = rho_new
    return add(x, d)


def lookup(index, rows, row):
    lane = index & 127
    group = index >> 7

    def tree(low, size):
        if size == 1:
            return jnp.take_along_axis(row(low), lane, axis=1, mode="promise_in_bounds")
        size //= 2
        return jnp.where((group & size) != 0, tree(low + size, size), tree(low, size))

    return tree(0, rows)


def gather_pair(fields, source, weight, pair, store):
    at = pl.ds(pl.multiple_of(8 * pair, 8), 8)
    index = source[at, :]
    wgt = weight[at, :]
    for f in range(7):

        def row(r):
            return jnp.broadcast_to(fields[f : f + 1, 128 * r : 128 * r + 128], (8, 128))

        store(f, lookup(index, 32, row) * wgt)


def scatter_pairs(arrived, target, total, pairs):
    iota = lax.broadcasted_iota(jnp.int32, (16, 128), 0).astype(jnp.int16)
    one = jnp.ones((16, 128), jnp.bfloat16)
    zero = jnp.zeros((16, 128), jnp.bfloat16)
    columns, values = [], []
    for slot, pair in pairs:
        for row in range(8):
            half, r = divmod(row, 4)
            cell = jnp.broadcast_to(target[pl.ds(8 * pair + row, 1), :], (16, 128))
            x = cell >> 11
            col = (((x & 1) << 7) + (cell & 127)).astype(jnp.int16)
            up = (((x >> 1) << 4) + ((cell >> 7) & 15)).astype(jnp.int16)
            columns.append(
                jnp.concatenate(
                    [jnp.where(iota == col - jnp.int16(16 * i), one, zero) for i in range(16)], axis=0
                )
            )
            here = [iota == up - jnp.int16(16 * i) for i in range(2)]
            high, low = [], []
            for f in range(7):
                val = jnp.broadcast_to(arrived[2 * slot + half, f, r : r + 1, :], (16, 128))
                top = val.astype(jnp.bfloat16)
                rest = (val - top.astype(jnp.float32)).astype(jnp.bfloat16)
                high += [jnp.where(m, top, zero) for m in here]
                low += [jnp.where(m, rest, zero) for m in here]
            values.append(jnp.concatenate(high + low, axis=0))
    total[...] += lax.dot_general(
        jnp.concatenate(values, axis=1),
        jnp.concatenate(columns, axis=1),
        (((1,), (1,)), ((), ())),
        preferred_element_type=jnp.float32,
    )


def cell_moduli(vals):
    phi = vals[0]
    mean = (vals[1] + vals[2] + vals[3]) / 3.0
    q2 = 1.5 * (
        (vals[1] - mean) ** 2
        + (vals[2] - mean) ** 2
        + (vals[3] - mean) ** 2
        + 2.0 * (vals[4] ** 2 + vals[5] ** 2 + vals[6] ** 2)
    )
    bulk = 1.6 * jnp.exp(-3.0 * phi) * (1.0 + 0.25 * jnp.tanh(mean))
    shear = 0.9 * jnp.exp(-2.0 * phi) / (1.0 + q2 / 0.5)
    soften = shear * q2 / (0.5 + q2)
    return bulk, shear, soften


def neighbour_sum(before, here, after):
    lane = lax.broadcasted_iota(jnp.int32, here.shape, 1)
    left = jnp.where(lane == 0, 0.0, pltpu.roll(here, 1, 1))
    right = jnp.where(lane == 127, 0.0, pltpu.roll(here, 127, 1))
    rows = here.shape[0]
    return (before + after) + (pltpu.roll(here, 1, 0) + pltpu.roll(here, rows - 1, 0)) + (left + right)


def whole_kernel(
    n_src,
    n_tgt,
    fields_in,
    source_in,
    weight_in,
    target_in,
    mass_in,
    leave_in,
    computed,
    landed,
    fields,
    source,
    weight,
    target,
    mass,
    leave,
    outgoing,
    arrived,
    total,
    resid,
    edge,
    beside,
    strips,
    table,
    packed,
    midway,
    projected,
    load_sem,
    send_sem,
    recv_sem,
    halo_send,
    halo_recv,
    across_send,
    across_recv,
    along_send,
    along_recv,
    keep_sem,
):
    owners = n_src * n_tgt
    pairs = owners // 2
    steps = pairs // STEP
    at_src, at_tgt = lax.axis_index("src"), lax.axis_index("tgt")
    me = at_src * n_tgt + at_tgt
    parity = me % 2

    def pair_at(step, sign):
        row, col = step % n_src, (step // n_src + step) % (n_tgt // 2)
        row = (at_src + sign * row + n_src) % n_src
        col = (at_tgt // 2 + sign * col + n_tgt // 2) % (n_tgt // 2)
        return row * (n_tgt // 2) + col

    loads = [
        pltpu.make_async_copy(a, b, load_sem.at[i])
        for i, (a, b) in enumerate(
            [
                (fields_in, fields),
                (source_in, source),
                (weight_in, weight),
                (target_in, target),
                (mass_in, mass),
                (leave_in, leave),
            ]
        )
    ]
    for load in loads:
        load.start()

    barrier = pltpu.get_barrier_semaphore()

    def gather(k):
        for u in range(STEP):
            slot = STEP * k + u

            def store(f, val):
                outgoing[2 * slot, f] = val[:4]
                outgoing[2 * slot + 1, f] = val[4:]

            gather_pair(fields, source, weight, pair_at(slot, 1), store)

    def copy(slot, half, landing):
        other = 2 * pair_at(slot, 1) + half
        return pltpu.make_async_remote_copy(
            src_ref=outgoing.at[2 * slot + half],
            dst_ref=arrived.at[2 * slot + landing],
            send_sem=send_sem.at[2 * slot + half],
            recv_sem=recv_sem.at[2 * slot + landing],
            device_id=(other // n_tgt, other % n_tgt),
            device_id_type=MESH,
        )

    def each_copy(k, act):
        for u in range(STEP):
            for half in range(2):
                slot = STEP * k + u
                if u == 0:

                    @pl.when((slot > 0) | (parity != half))
                    def _():
                        act(slot, half)

                else:
                    act(slot, half)

    def launch(k):
        each_copy(k, lambda slot, half: copy(slot, half, parity).start())

    def take(k):
        each_copy(k, lambda slot, half: copy(slot, half, half).wait_recv())

    def scatter(k):
        scatter_pairs(
            arrived,
            target,
            total,
            [(STEP * k + u, pair_at(STEP * k + u, -1)) for u in range(STEP)],
        )

    def greet_row(k, carry):
        row = lax.rem(at_src + lax.rem(k + n_src // 2 - 2, n_src - 1) + 1, n_src)
        for j in range(n_tgt):
            pl.semaphore_signal(
                barrier, inc=1, device_id=(row, lax.rem(at_tgt + j, n_tgt)), device_id_type=MESH
            )
        return carry

    lax.fori_loop(1, n_src, greet_row, 0)
    for j in range(1, n_tgt):
        pl.semaphore_signal(
            barrier, inc=1, device_id=(at_src, lax.rem(at_tgt + j, n_tgt)), device_id_type=MESH
        )
    total[...] = jnp.zeros_like(total)

    @pl.when(at_src == 0)
    def _():
        beside[0] = jnp.zeros_like(beside[0])
        strips[0] = jnp.zeros_like(strips[0])

    @pl.when(at_src == n_src - 1)
    def _():
        beside[1] = jnp.zeros_like(beside[1])
        strips[2] = jnp.zeros_like(strips[2])

    for side, end in ((0, n_tgt - 1), (1, 0)):

        @pl.when(at_tgt == end)
        def _():
            for block in range(3):
                strips[block, side] = jnp.zeros_like(strips[block, side])

    for load in loads:
        load.wait()

    def gather_only(k, carry):
        gather(k)
        return carry

    def launch_only(k, carry):
        launch(k)
        return carry

    def gather_launch(k, carry):
        gather(k)
        launch(k)
        return carry

    def gather_scatter(k, carry):
        take(k)
        gather(k + AHEAD)
        scatter(k)
        launch(k + AHEAD)
        return carry

    def scatter_only(k, carry):
        take(k)
        scatter(k)
        return carry

    lax.fori_loop(0, GREET, gather_only, 0)
    pl.semaphore_wait(barrier, owners - 1)
    lax.fori_loop(0, GREET, launch_only, 0)
    arrived[parity] = outgoing[parity]
    lax.fori_loop(GREET, AHEAD, gather_launch, 0)
    lax.fori_loop(0, steps - AHEAD, gather_scatter, 0)
    lax.fori_loop(steps - AHEAD, steps, scatter_only, 0)

    inverse = [lax.rsqrt(mass[x]) for x in range(4)]
    def halo(part, i):
        da, db = TURNS[i]
        span = pl.ds(*PARTS[part])
        if db == 0:
            src, dst = resid.at[span], beside.at[0 if da == 1 else 1, span]
        else:
            side = 1 if db == 1 else 0
            src, dst = edge.at[side, span], strips.at[1 - da, side, span]
        return pltpu.make_async_remote_copy(
            src_ref=src,
            dst_ref=dst,
            send_sem=halo_send.at[8 * part + i],
            recv_sem=halo_recv.at[8 * part + i],
            device_id=((at_src + da + n_src) % n_src, (at_tgt + db + n_tgt) % n_tgt),
            device_id_type=MESH,
        )

    def inside(i, sign):
        da, db = TURNS[i]
        a, b = at_src + sign * da, at_tgt + sign * db
        return (a >= 0) & (a < n_src) & (b >= 0) & (b < n_tgt)

    def each_halo(part, sign, act):
        for i in range(8):

            @pl.when(inside(i, sign))
            def _():
                act(halo(part, i))

    for part, (first, count) in enumerate(PARTS):
        for f in range(first, first + count):
            for x in range(4):
                rows = pl.ds(32 * f + 16 * (x // 2), 16)
                lower = pl.ds(224 + 32 * f + 16 * (x // 2), 16)
                cols = pl.ds(128 * (x % 2), 128)
                val = (total[rows, cols] + total[lower, cols]) * inverse[x]
                resid[f, x] = val
                edge[0, f, x] = val[:4]
                edge[1, f, x] = val[12:]
        each_halo(part, 1, lambda sent: sent.start())

    def drain_copies(k, carry):
        each_copy(k, lambda slot, half: copy(slot, half, half).wait_send())
        return carry

    lax.fori_loop(0, steps, drain_copies, 0)
    coefs = chebyshev_coefficients()
    row_id = lax.broadcasted_iota(jnp.int32, (24, 128), 0)
    has_next = (at_tgt < n_tgt - 1).astype(jnp.float32)
    has_last = (at_tgt > 0).astype(jnp.float32)
    valid = jnp.where(row_id < 16, 1.0, jnp.where(row_id < 20, has_next, has_last))
    valid_of = [
        valid * (at_src > 0).astype(jnp.float32),
        valid,
        valid * (at_src < n_src - 1).astype(jnp.float32),
    ]

    def sweeps(f, carry):
        planes = []
        for p in range(12):
            block, q = divmod(p, 4)
            main = resid[f, q] if block == 1 else beside[block // 2, f, q]
            planes.append(jnp.concatenate([main, strips[block, 0, f, q], strips[block, 1, f, q]], axis=0))
        state = [coefs[ITERS] * v for v in planes]
        for depth in range(1, ITERS + 1):
            fresh = list(state)
            for p in range(depth, 12 - depth):
                val = neighbour_sum(state[p - 1], state[p], state[p + 1]) + coefs[ITERS - depth] * planes[p]
                fresh[p] = val if depth == ITERS else val * valid_of[p // 4]
            state = fresh
        for x in range(4):
            projected[f, x] = state[4 + x][:16] * inverse[x]
        return carry

    for part, (first, count) in enumerate(PARTS):
        each_halo(part, -1, lambda came: came.wait_recv())
        lax.fori_loop(first, first + count, sweeps, 0)

    keep = pltpu.make_async_copy(projected, computed, keep_sem)
    keep.start()

    for x in range(4):
        for h in range(2):
            got = cell_moduli([projected[f, x, 8 * h : 8 * h + 8, :] for f in range(7)])
            for m in range(3):
                table[m, 16 * x + 8 * h : 16 * x + 8 * h + 8, :] = got[m]

    lower_half = lax.broadcasted_iota(jnp.int32, (8, 128), 1) < 64

    def swapped(v):
        return pltpu.roll(v, 64, 1)

    def across(k):
        other = (at_src + k) % n_src
        return pltpu.make_async_remote_copy(
            src_ref=packed.at[other],
            dst_ref=midway.at[at_src],
            send_sem=across_send.at[k],
            recv_sem=across_recv.at[k],
            device_id=(other, at_tgt),
            device_id_type=MESH,
        )

    def along(k):
        other = (at_tgt + k) % n_tgt
        return pltpu.make_async_remote_copy(
            src_ref=midway.at[:, other],
            dst_ref=landed.at[:, at_tgt],
            send_sem=along_send.at[k],
            recv_sem=along_recv.at[k],
            device_id=(at_src, other),
            device_id_type=MESH,
        )

    def send_group(step, carry):
        group = (step + at_src) % n_src
        index = leave[pl.ds(pl.multiple_of(8 * group, 8), 8), :]
        bulk, shear, soften = [
            lookup(index, 64, lambda r: jnp.broadcast_to(table[m, r : r + 1, :], (8, 128)))
            for m in range(3)
        ]
        even = jnp.full((8, 128), parity, jnp.int32) == 0
        one = jnp.where(even, bulk, shear)
        two = jnp.where(even, shear, bulk)
        soft_swapped = swapped(soften)
        blocks = [
            [jnp.where(lower_half, one, swapped(two)), jnp.where(even, soften, soft_swapped)],
            [jnp.where(lower_half, swapped(one), two), jnp.where(even, soft_swapped, soften)],
        ]
        for i in range(8):
            for half in range(2):
                for r in range(2):
                    packed[group, 2 * i + half, r : r + 1, :] = blocks[half][r][i : i + 1, :]

        @pl.when(step < n_src)
        def _():
            across(step).start()

        return carry

    lax.fori_loop(1, n_src + 1, send_group, 0)
    midway[at_src] = packed[at_src]
    for k in range(1, n_src):
        across(k).wait_recv()
    for k in range(1, n_tgt):
        along(k).start()
    landed[:, at_tgt] = midway[:, at_tgt]
    for k in range(1, n_tgt):
        along(k).wait_recv()

    for k in range(1, n_src):
        across(k).wait_send()
    for k in range(1, n_tgt):
        along(k).wait_send()
    keep.wait()
    for part in range(len(PARTS)):
        each_halo(part, 1, lambda sent: sent.wait_send())


def place_kernel(landed, place, computed, projected, moduli, passing, sem):
    bring = pltpu.make_async_copy(computed, passing, sem.at[0])
    keep = pltpu.make_async_copy(passing, projected, sem.at[1])
    bring.start()
    lower_half = lax.broadcasted_iota(jnp.int32, (8, 128), 1) < 64

    def fill(step, carry):
        index = place[pl.ds(pl.multiple_of(8 * step, 8), 8), :]

        def row(m, r):
            first, second = [
                jnp.broadcast_to(landed[r // 8, (2 * r + i) % 16, m // 2 : m // 2 + 1, :], (8, 128))
                for i in range(2)
            ]
            return jnp.where(lower_half, second, first) if m == 1 else jnp.where(lower_half, first, second)

        for m in range(3):
            at = index ^ 64 if m == 1 else index
            got = lookup(at, 64, functools.partial(row, m))
            for i in range(8):
                moduli[m : m + 1, pl.ds(pl.multiple_of(1024 * step + 128 * i, 128), 128)] = got[i : i + 1]
        return carry

    lax.fori_loop(0, 4, fill, 0)
    bring.wait()
    keep.start()
    lax.fori_loop(4, 8, fill, 0)
    keep.wait()


def on_device(
    source_fields, slot_source, slot_weight, slot_target, cell_mass, send_order, place_order
):
    n_src = lax.axis_size("src")
    n_tgt = lax.axis_size("tgt")
    owners = n_src * n_tgt
    hx, hy, hz = cell_mass.shape
    cells = hx * hy * hz
    f32, i32 = jnp.float32, jnp.int32
    args = (
        source_fields,
        slot_source.reshape(4 * owners, 128),
        slot_weight.reshape(4 * owners, 128),
        slot_target.reshape(4 * owners, 128),
        cell_mass,
        send_order.reshape(cells // 128, 128),
    )
    vmem = pl.BlockSpec(memory_space=pltpu.VMEM)
    far = pl.BlockSpec(memory_space=pl.ANY)
    computed, landed = pl.pallas_call(
        functools.partial(whole_kernel, n_src, n_tgt),
        out_shape=(
            jax.ShapeDtypeStruct((7, hx, hy, hz), f32),
            jax.ShapeDtypeStruct((n_src, n_tgt, 2, 128), f32),
        ),
        in_specs=[pl.BlockSpec(memory_space=pltpu.HBM)] * len(args),
        out_specs=(far, vmem),
        scratch_shapes=[pltpu.VMEM(a.shape, a.dtype) for a in args]
        + [
            pltpu.VMEM((owners, 7, 4, 128), f32),
            pltpu.VMEM((owners, 7, 4, 128), f32),
            pltpu.VMEM((448, 256), f32),
            pltpu.VMEM((7, hx, hy, hz), f32),
            pltpu.VMEM((2, 7, hx, 4, hz), f32),
            pltpu.VMEM((2, 7, hx, hy, hz), f32),
            pltpu.VMEM((3, 2, 7, hx, 4, hz), f32),
            pltpu.VMEM((3, cells // 128, 128), f32),
            pltpu.VMEM((n_src, n_tgt, 2, 128), f32),
            pltpu.VMEM((n_src, n_tgt, 2, 128), f32),
            pltpu.VMEM((7, hx, hy, hz), f32),
            pltpu.SemaphoreType.DMA((len(args),)),
            pltpu.SemaphoreType.DMA((owners,)),
            pltpu.SemaphoreType.DMA((owners,)),
            pltpu.SemaphoreType.DMA((8 * len(PARTS),)),
            pltpu.SemaphoreType.DMA((8 * len(PARTS),)),
            pltpu.SemaphoreType.DMA((n_src,)),
            pltpu.SemaphoreType.DMA((n_src,)),
            pltpu.SemaphoreType.DMA((n_tgt,)),
            pltpu.SemaphoreType.DMA((n_tgt,)),
            pltpu.SemaphoreType.DMA,
        ],
        compiler_params=pltpu.CompilerParams(
            collective_id=0, has_side_effects=True, vmem_limit_bytes=60 << 20
        ),
    )(*args)
    return pl.pallas_call(
        place_kernel,
        out_shape=(
            jax.ShapeDtypeStruct((7, hx, hy, hz), f32),
            jax.ShapeDtypeStruct((3, cells), f32),
        ),
        in_specs=(vmem, vmem, far),
        out_specs=(far, vmem),
        scratch_shapes=[pltpu.VMEM((7, hx, hy, hz), f32), pltpu.SemaphoreType.DMA((2,))],
    )(landed, place_order.reshape(cells // 128, 128), computed)


def solution(mesh):
    placed = (
        P(None, ("src", "tgt")),
        P(("src", "tgt")),
        P(("src", "tgt")),
        P(("src", "tgt")),
        P("src", "tgt", None),
        P(("src", "tgt"), None),
        P(("src", "tgt"), None),
    )
    return jax.shard_map(
        on_device,
        mesh=mesh,
        in_specs=placed,
        out_specs=(P(None, "src", "tgt", None), P(None, ("src", "tgt"))),
        check_vma=False,
    )
```

```python
import functools

import jax
import jax.numpy as jnp
from jax import lax
from jax.experimental import pallas as pl
from jax.experimental.pallas import tpu as pltpu
from jax.sharding import PartitionSpec as P

ITERS = 4
MESH = pl.DeviceIdType.MESH
STEP = 4
GREET = 2
AHEAD = 6
PARTS = [(0, 1), (1, 2), (3, 2), (5, 2)]
TURNS = [(1, 0), (-1, 0), (1, 1), (1, -1), (-1, 1), (-1, -1), (0, 1), (0, -1)]


def chebyshev_coefficients():
    def add(p, q, scale=1.0):
        size = max(len(p), len(q))
        p, q = (list(p) + [0.0] * (size - len(p)), list(q) + [0.0] * (size - len(q)))
        return [u + scale * v for u, v in zip(p, q)]

    theta, delta = 1.0, 0.75
    sigma = theta / delta
    rho = 1.0 / sigma
    x, r, d = ([0.0], [1.0], [1.0 / theta])
    for _ in range(ITERS):
        image = add(d, [0.0] + [0.125 * v for v in d])
        x = add(x, d)
        r = add(r, image, -1.0)
        rho_new = 1.0 / (2.0 * sigma - rho)
        d = add([rho_new * rho * v for v in d], [2.0 * rho_new / delta * v for v in r])
        rho = rho_new
    return add(x, d)


def lookup(index, rows, row):
    lane = index & 127
    group = index >> 7

    def tree(low, size):
        if size == 1:
            return jnp.take_along_axis(row(low), lane, axis=1, mode="promise_in_bounds")
        size //= 2
        return jnp.where((group & size) != 0, tree(low + size, size), tree(low, size))

    return tree(0, rows)


def gather_pair(fields, source, weight, pair, store):
    at = pl.ds(pl.multiple_of(8 * pair, 8), 8)
    index = source[at, :]
    wgt = weight[at, :]
    for f in range(7):

        def row(r):
            return jnp.broadcast_to(fields[f : f + 1, 128 * r : 128 * r + 128], (8, 128))

        store(f, lookup(index, 32, row) * wgt)


def scatter_pairs(arrived, target, total, pairs):
    iota = lax.broadcasted_iota(jnp.int32, (16, 128), 0).astype(jnp.int16)
    one = jnp.ones((16, 128), jnp.bfloat16)
    zero = jnp.zeros((16, 128), jnp.bfloat16)
    columns, values = [], []
    for slot, pair in pairs:
        for row in range(8):
            half, r = divmod(row, 4)
            cell = jnp.broadcast_to(target[pl.ds(8 * pair + row, 1), :], (16, 128))
            x = cell >> 11
            col = (((x & 1) << 7) + (cell & 127)).astype(jnp.int16)
            up = (((x >> 1) << 4) + ((cell >> 7) & 15)).astype(jnp.int16)
            columns.append(
                jnp.concatenate(
                    [jnp.where(iota == col - jnp.int16(16 * i), one, zero) for i in range(16)], axis=0
                )
            )
            here = [iota == up - jnp.int16(16 * i) for i in range(2)]
            high, low = [], []
            for f in range(7):
                val = jnp.broadcast_to(arrived[2 * slot + half, f, r : r + 1, :], (16, 128))
                top = val.astype(jnp.bfloat16)
                rest = (val - top.astype(jnp.float32)).astype(jnp.bfloat16)
                high += [jnp.where(m, top, zero) for m in here]
                low += [jnp.where(m, rest, zero) for m in here]
            values.append(jnp.concatenate(high + low, axis=0))
    total[...] += lax.dot_general(
        jnp.concatenate(values, axis=1),
        jnp.concatenate(columns, axis=1),
        (((1,), (1,)), ((), ())),
        preferred_element_type=jnp.float32,
    )


def cell_moduli(vals):
    phi = vals[0]
    mean = (vals[1] + vals[2] + vals[3]) / 3.0
    q2 = 1.5 * (
        (vals[1] - mean) ** 2
        + (vals[2] - mean) ** 2
        + (vals[3] - mean) ** 2
        + 2.0 * (vals[4] ** 2 + vals[5] ** 2 + vals[6] ** 2)
    )
    bulk = 1.6 * jnp.exp(-3.0 * phi) * (1.0 + 0.25 * jnp.tanh(mean))
    shear = 0.9 * jnp.exp(-2.0 * phi) / (1.0 + q2 / 0.5)
    soften = shear * q2 / (0.5 + q2)
    return bulk, shear, soften


def neighbour_sum(before, here, after):
    lane = lax.broadcasted_iota(jnp.int32, here.shape, 1)
    left = jnp.where(lane == 0, 0.0, pltpu.roll(here, 1, 1))
    right = jnp.where(lane == 127, 0.0, pltpu.roll(here, 127, 1))
    rows = here.shape[0]
    return (before + after) + (pltpu.roll(here, 1, 0) + pltpu.roll(here, rows - 1, 0)) + (left + right)


def whole_kernel(
    n_src,
    n_tgt,
    fields_in,
    source_in,
    weight_in,
    target_in,
    mass_in,
    leave_in,
    computed,
    landed,
    fields,
    source,
    weight,
    target,
    mass,
    leave,
    outgoing,
    arrived,
    total,
    resid,
    edge,
    beside,
    strips,
    table,
    packed,
    midway,
    projected,
    load_sem,
    send_sem,
    recv_sem,
    halo_send,
    halo_recv,
    across_send,
    across_recv,
    along_send,
    along_recv,
    keep_sem,
):
    owners = n_src * n_tgt
    pairs = owners // 2
    steps = pairs // STEP
    at_src, at_tgt = lax.axis_index("src"), lax.axis_index("tgt")
    me = at_src * n_tgt + at_tgt
    parity = me % 2

    def pair_at(step, sign):
        row, col = step % n_src, (step // n_src + step) % (n_tgt // 2)
        row = (at_src + sign * row + n_src) % n_src
        col = (at_tgt // 2 + sign * col + n_tgt // 2) % (n_tgt // 2)
        return row * (n_tgt // 2) + col

    loads = [
        pltpu.make_async_copy(a, b, load_sem.at[i])
        for i, (a, b) in enumerate(
            [
                (fields_in, fields),
                (source_in, source),
                (weight_in, weight),
                (target_in, target),
                (mass_in, mass),
                (leave_in, leave),
            ]
        )
    ]
    for load in loads:
        load.start()

    barrier = pltpu.get_barrier_semaphore()

    def gather(k):
        for u in range(STEP):
            slot = STEP * k + u

            def store(f, val):
                outgoing[2 * slot, f] = val[:4]
                outgoing[2 * slot + 1, f] = val[4:]

            gather_pair(fields, source, weight, pair_at(slot, 1), store)

    def copy(slot, half, landing):
        other = 2 * pair_at(slot, 1) + half
        return pltpu.make_async_remote_copy(
            src_ref=outgoing.at[2 * slot + half],
            dst_ref=arrived.at[2 * slot + landing],
            send_sem=send_sem.at[2 * slot + half],
            recv_sem=recv_sem.at[2 * slot + landing],
            device_id=(other // n_tgt, other % n_tgt),
            device_id_type=MESH,
        )

    def each_copy(k, act):
        for u in range(STEP):
            for half in range(2):
                slot = STEP * k + u
                if u == 0:

                    @pl.when((slot > 0) | (parity != half))
                    def _():
                        act(slot, half)

                else:
                    act(slot, half)

    def launch(k):
        each_copy(k, lambda slot, half: copy(slot, half, parity).start())

    def take(k):
        each_copy(k, lambda slot, half: copy(slot, half, half).wait_recv())

    def scatter(k):
        scatter_pairs(
            arrived,
            target,
            total,
            [(STEP * k + u, pair_at(STEP * k + u, -1)) for u in range(STEP)],
        )

    def greet_row(k, carry):
        row = lax.rem(at_src + lax.rem(k + n_src // 2 - 2, n_src - 1) + 1, n_src)
        for j in range(n_tgt):
            pl.semaphore_signal(
                barrier, inc=1, device_id=(row, lax.rem(at_tgt + j, n_tgt)), device_id_type=MESH
            )
        return carry

    lax.fori_loop(1, n_src, greet_row, 0)
    for j in range(1, n_tgt):
        pl.semaphore_signal(
            barrier, inc=1, device_id=(at_src, lax.rem(at_tgt + j, n_tgt)), device_id_type=MESH
        )
    total[...] = jnp.zeros_like(total)

    @pl.when(at_src == 0)
    def _():
        beside[0] = jnp.zeros_like(beside[0])
        strips[0] = jnp.zeros_like(strips[0])

    @pl.when(at_src == n_src - 1)
    def _():
        beside[1] = jnp.zeros_like(beside[1])
        strips[2] = jnp.zeros_like(strips[2])

    for side, end in ((0, n_tgt - 1), (1, 0)):

        @pl.when(at_tgt == end)
        def _():
            for block in range(3):
                strips[block, side] = jnp.zeros_like(strips[block, side])

    for load in loads:
        load.wait()

    def gather_only(k, carry):
        gather(k)
        return carry

    def launch_only(k, carry):
        launch(k)
        return carry

    def gather_launch(k, carry):
        gather(k)
        launch(k)
        return carry

    def gather_scatter(k, carry):
        take(k)
        gather(k + AHEAD)
        scatter(k)
        launch(k + AHEAD)
        return carry

    def scatter_only(k, carry):
        take(k)
        scatter(k)
        return carry

    lax.fori_loop(0, GREET, gather_only, 0)
    pl.semaphore_wait(barrier, owners - 1)
    lax.fori_loop(0, GREET, launch_only, 0)
    arrived[parity] = outgoing[parity]
    lax.fori_loop(GREET, AHEAD, gather_launch, 0)
    lax.fori_loop(0, steps - AHEAD, gather_scatter, 0)
    lax.fori_loop(steps - AHEAD, steps, scatter_only, 0)

    inverse = [lax.rsqrt(mass[x]) for x in range(4)]
    def halo(part, i):
        da, db = TURNS[i]
        span = pl.ds(*PARTS[part])
        if db == 0:
            src, dst = resid.at[span], beside.at[0 if da == 1 else 1, span]
        else:
            side = 1 if db == 1 else 0
            src, dst = edge.at[side, span], strips.at[1 - da, side, span]
        return pltpu.make_async_remote_copy(
            src_ref=src,
            dst_ref=dst,
            send_sem=halo_send.at[8 * part + i],
            recv_sem=halo_recv.at[8 * part + i],
            device_id=((at_src + da + n_src) % n_src, (at_tgt + db + n_tgt) % n_tgt),
            device_id_type=MESH,
        )

    def inside(i, sign):
        da, db = TURNS[i]
        a, b = at_src + sign * da, at_tgt + sign * db
        return (a >= 0) & (a < n_src) & (b >= 0) & (b < n_tgt)

    def each_halo(part, sign, act):
        for i in range(8):

            @pl.when(inside(i, sign))
            def _():
                act(halo(part, i))

    for part, (first, count) in enumerate(PARTS):
        for f in range(first, first + count):
            for x in range(4):
                rows = pl.ds(32 * f + 16 * (x // 2), 16)
                lower = pl.ds(224 + 32 * f + 16 * (x // 2), 16)
                cols = pl.ds(128 * (x % 2), 128)
                val = (total[rows, cols] + total[lower, cols]) * inverse[x]
                resid[f, x] = val
                edge[0, f, x] = val[:4]
                edge[1, f, x] = val[12:]
        each_halo(part, 1, lambda sent: sent.start())

    def drain_copies(k, carry):
        each_copy(k, lambda slot, half: copy(slot, half, half).wait_send())
        return carry

    lax.fori_loop(0, steps, drain_copies, 0)
    coefs = chebyshev_coefficients()
    row_id = lax.broadcasted_iota(jnp.int32, (24, 128), 0)
    has_next = (at_tgt < n_tgt - 1).astype(jnp.float32)
    has_last = (at_tgt > 0).astype(jnp.float32)
    valid = jnp.where(row_id < 16, 1.0, jnp.where(row_id < 20, has_next, has_last))
    valid_of = [
        valid * (at_src > 0).astype(jnp.float32),
        valid,
        valid * (at_src < n_src - 1).astype(jnp.float32),
    ]

    def sweeps(f, carry):
        planes = []
        for p in range(12):
            block, q = divmod(p, 4)
            main = resid[f, q] if block == 1 else beside[block // 2, f, q]
            planes.append(jnp.concatenate([main, strips[block, 0, f, q], strips[block, 1, f, q]], axis=0))
        state = [coefs[ITERS] * v for v in planes]
        for depth in range(1, ITERS + 1):
            fresh = list(state)
            for p in range(depth, 12 - depth):
                val = neighbour_sum(state[p - 1], state[p], state[p + 1]) + coefs[ITERS - depth] * planes[p]
                fresh[p] = val if depth == ITERS else val * valid_of[p // 4]
            state = fresh
        for x in range(4):
            projected[f, x] = state[4 + x][:16] * inverse[x]
        return carry

    for part, (first, count) in enumerate(PARTS):
        each_halo(part, -1, lambda came: came.wait_recv())
        lax.fori_loop(first, first + count, sweeps, 0)

    keep = pltpu.make_async_copy(projected, computed, keep_sem)
    keep.start()

    for x in range(4):
        for h in range(2):
            got = cell_moduli([projected[f, x, 8 * h : 8 * h + 8, :] for f in range(7)])
            for m in range(3):
                table[m, 16 * x + 8 * h : 16 * x + 8 * h + 8, :] = got[m]

    lower_half = lax.broadcasted_iota(jnp.int32, (8, 128), 1) < 64

    def swapped(v):
        return pltpu.roll(v, 64, 1)

    def across(k):
        other = (at_src + k) % n_src
        return pltpu.make_async_remote_copy(
            src_ref=packed.at[other],
            dst_ref=midway.at[at_src],
            send_sem=across_send.at[k],
            recv_sem=across_recv.at[k],
            device_id=(other, at_tgt),
            device_id_type=MESH,
        )

    def along(k):
        other = (at_tgt + k) % n_tgt
        return pltpu.make_async_remote_copy(
            src_ref=midway.at[:, other],
            dst_ref=landed.at[:, at_tgt],
            send_sem=along_send.at[k],
            recv_sem=along_recv.at[k],
            device_id=(at_src, other),
            device_id_type=MESH,
        )

    def send_group(step, carry):
        group = (step + at_src) % n_src
        index = leave[pl.ds(pl.multiple_of(8 * group, 8), 8), :]
        bulk, shear, soften = [
            lookup(index, 64, lambda r: jnp.broadcast_to(table[m, r : r + 1, :], (8, 128)))
            for m in range(3)
        ]
        even = jnp.full((8, 128), parity, jnp.int32) == 0
        one = jnp.where(even, bulk, shear)
        two = jnp.where(even, shear, bulk)
        soft_swapped = swapped(soften)
        blocks = [
            [jnp.where(lower_half, one, swapped(two)), jnp.where(even, soften, soft_swapped)],
            [jnp.where(lower_half, swapped(one), two), jnp.where(even, soft_swapped, soften)],
        ]
        for i in range(8):
            for half in range(2):
                for r in range(2):
                    packed[group, 2 * i + half, r : r + 1, :] = blocks[half][r][i : i + 1, :]

        @pl.when(step < n_src)
        def _():
            across(step).start()

        return carry

    lax.fori_loop(1, n_src + 1, send_group, 0)
    midway[at_src] = packed[at_src]
    for k in range(1, n_src):
        across(k).wait_recv()
    for k in range(1, n_tgt):
        along(k).start()
    landed[:, at_tgt] = midway[:, at_tgt]
    for k in range(1, n_tgt):
        along(k).wait_recv()

    for k in range(1, n_src):
        across(k).wait_send()
    for k in range(1, n_tgt):
        along(k).wait_send()
    keep.wait()
    for part in range(len(PARTS)):
        each_halo(part, 1, lambda sent: sent.wait_send())


def place_kernel(landed, place, computed, projected, moduli, passing, sem):
    bring = pltpu.make_async_copy(computed, passing, sem.at[0])
    keep = pltpu.make_async_copy(passing, projected, sem.at[1])
    bring.start()
    lower_half = lax.broadcasted_iota(jnp.int32, (8, 128), 1) < 64

    def fill(step, carry):
        index = place[pl.ds(pl.multiple_of(8 * step, 8), 8), :]

        def row(m, r):
            first, second = [
                jnp.broadcast_to(landed[r // 8, (2 * r + i) % 16, m // 2 : m // 2 + 1, :], (8, 128))
                for i in range(2)
            ]
            return jnp.where(lower_half, second, first) if m == 1 else jnp.where(lower_half, first, second)

        for m in range(3):
            at = index ^ 64 if m == 1 else index
            got = lookup(at, 64, functools.partial(row, m))
            for i in range(8):
                moduli[m : m + 1, pl.ds(pl.multiple_of(1024 * step + 128 * i, 128), 128)] = got[i : i + 1]
        return carry

    lax.fori_loop(0, 4, fill, 0)
    bring.wait()
    keep.start()
    lax.fori_loop(4, 8, fill, 0)
    keep.wait()


def on_device(
    source_fields, slot_source, slot_weight, slot_target, cell_mass, send_order, place_order
):
    n_src = lax.axis_size("src")
    n_tgt = lax.axis_size("tgt")
    owners = n_src * n_tgt
    hx, hy, hz = cell_mass.shape
    cells = hx * hy * hz
    f32, i32 = jnp.float32, jnp.int32
    args = (
        source_fields,
        slot_source.reshape(4 * owners, 128),
        slot_weight.reshape(4 * owners, 128),
        slot_target.reshape(4 * owners, 128),
        cell_mass,
        send_order.reshape(cells // 128, 128),
    )
    vmem = pl.BlockSpec(memory_space=pltpu.VMEM)
    far = pl.BlockSpec(memory_space=pl.ANY)
    computed, landed = pl.pallas_call(
        functools.partial(whole_kernel, n_src, n_tgt),
        out_shape=(
            jax.ShapeDtypeStruct((7, hx, hy, hz), f32),
            jax.ShapeDtypeStruct((n_src, n_tgt, 2, 128), f32),
        ),
        in_specs=[pl.BlockSpec(memory_space=pltpu.HBM)] * len(args),
        out_specs=(far, vmem),
        scratch_shapes=[pltpu.VMEM(a.shape, a.dtype) for a in args]
        + [
            pltpu.VMEM((owners, 7, 4, 128), f32),
            pltpu.VMEM((owners, 7, 4, 128), f32),
            pltpu.VMEM((448, 256), f32),
            pltpu.VMEM((7, hx, hy, hz), f32),
            pltpu.VMEM((2, 7, hx, 4, hz), f32),
            pltpu.VMEM((2, 7, hx, hy, hz), f32),
            pltpu.VMEM((3, 2, 7, hx, 4, hz), f32),
            pltpu.VMEM((3, cells // 128, 128), f32),
            pltpu.VMEM((n_src, n_tgt, 2, 128), f32),
            pltpu.VMEM((n_src, n_tgt, 2, 128), f32),
            pltpu.VMEM((7, hx, hy, hz), f32),
            pltpu.SemaphoreType.DMA((len(args),)),
            pltpu.SemaphoreType.DMA((owners,)),
            pltpu.SemaphoreType.DMA((owners,)),
            pltpu.SemaphoreType.DMA((8 * len(PARTS),)),
            pltpu.SemaphoreType.DMA((8 * len(PARTS),)),
            pltpu.SemaphoreType.DMA((n_src,)),
            pltpu.SemaphoreType.DMA((n_src,)),
            pltpu.SemaphoreType.DMA((n_tgt,)),
            pltpu.SemaphoreType.DMA((n_tgt,)),
            pltpu.SemaphoreType.DMA,
        ],
        compiler_params=pltpu.CompilerParams(
            collective_id=0, has_side_effects=True, vmem_limit_bytes=60 << 20
        ),
    )(*args)
    return pl.pallas_call(
        place_kernel,
        out_shape=(
            jax.ShapeDtypeStruct((7, hx, hy, hz), f32),
            jax.ShapeDtypeStruct((3, cells), f32),
        ),
        in_specs=(vmem, vmem, far),
        out_specs=(far, vmem),
        scratch_shapes=[pltpu.VMEM((7, hx, hy, hz), f32), pltpu.SemaphoreType.DMA((2,))],
    )(landed, place_order.reshape(cells // 128, 128), computed)


def solution(mesh):
    placed = (
        P(None, ("src", "tgt")),
        P(("src", "tgt")),
        P(("src", "tgt")),
        P(("src", "tgt")),
        P("src", "tgt", None),
        P(("src", "tgt"), None),
        P(("src", "tgt"), None),
    )
    return jax.shard_map(
        on_device,
        mesh=mesh,
        in_specs=placed,
        out_specs=(P(None, "src", "tgt", None), P(None, ("src", "tgt"))),
        check_vma=False,
    )
```
